128 devices in a mesh: ctx: 16 (over y, x), head: 8 (over z, core).
Axes of the slice: x: 4, y: 4, z: 4, core: 2. Of those that a mesh axis runs over, the one named last changes fastest.
Arguments:
- signal: bfloat16 [32768, 8192], P('ctx', 'head'), may hold values from -6 to 6
- log_decay: float32 [128, 32768], P('head', 'ctx'), may hold values from -0.61 to 0, as said below
- state_in: bfloat16 [32768, 1024], P(('ctx', 'head')), may hold values from -0.14941406 to 0.14941406
- state_out: bfloat16 [32768, 1024], P(('ctx', 'head')), may hold values from -0.14941406 to 0.14941406
- cotangent: bfloat16 [32768, 8192], P('ctx', 'head'), may hold values from -0.59765625 to 0.59765625
Outputs:
- output: bfloat16 [32768, 8192], P('ctx', 'head')
- grad_signal: bfloat16 [32768, 8192], P('ctx', 'head')
- grad_state_in: bfloat16 [32768, 1024], P(('ctx', 'head'))
- grad_state_out: bfloat16 [32768, 1024], P(('ctx', 'head'))
- grad_decay: float32 [128, 32768], P('head', 'ctx')
The draws below stay inside these ranges and needn't reach their ends.
Inputs may be any that keep to these rules, and one draw needn't show every extreme that they name: `log_decay`: negative everywhere.
All inputs are finite; a program needn't handle non-finite values.
Results may differ from the reference program's by a relative error of at most 0.0064.
Values may be sent and summed in bfloat16 or wider, within the bound.
No kernel may reach another device: no remote copies, remote signals or barrier semaphores. Data moves between devices by JAX's collectives and lax.ppermute only.
A program may use at most 128 MiB of HBM per device.

```python
import math
import jax
import jax.numpy as jnp
from jax import lax

HEAD_COUNT = 128
P_SIZE = 64
N = 128
G = 8
Q = 256
TOK_DEV = 2048
SEQUENCE_LENGTH = 32768


def draw_log_decay(key, part):
    key = jax.random.fold_in(key, 7)
    random_split_keys = jax.random.split(key, 7)
    fast_share = 0.5
    fast_heads = jax.random.uniform(random_split_keys[0], (HEAD_COUNT, 1)) < fast_share
    fast_rate = jnp.exp(jax.random.uniform(random_split_keys[1], (HEAD_COUNT, 1), minval=math.log(1.0 / 50.0), maxval=math.log(1.0 / 30.0)))
    slow_rate = jax.random.uniform(random_split_keys[2], (HEAD_COUNT, 1), minval=0.2, maxval=0.8) / SEQUENCE_LENGTH
    baseline_decay_rate = jnp.where(fast_heads, fast_rate, slow_rate)
    jitter_amplitude = jax.random.uniform(random_split_keys[3], (HEAD_COUNT, SEQUENCE_LENGTH), minval=0.5, maxval=1.5)
    device_blocks = SEQUENCE_LENGTH // TOK_DEV
    block_multiplier = jnp.exp(jax.random.uniform(random_split_keys[4], (HEAD_COUNT, device_blocks), minval=-0.7, maxval=0.7))
    block_multiplier = jnp.repeat(block_multiplier, TOK_DEV, axis=1)
    spike_positions = jax.random.uniform(random_split_keys[5], (HEAD_COUNT, SEQUENCE_LENGTH)) < 3.0 / SEQUENCE_LENGTH
    spike_length = jax.random.uniform(random_split_keys[6], (HEAD_COUNT, SEQUENCE_LENGTH), minval=0.22, maxval=0.5)
    spike_events = jnp.where(spike_positions, spike_length, 0.0)
    return (-(baseline_decay_rate * jitter_amplitude * block_multiplier + spike_events)).astype(jnp.float32)


def block_levels(own_key, shape, shards, least, high):
    level, own = 1.0, jax.random.fold_in(own_key, 6)
    for dim, parts in shards:
        draws = jnp.exp(jax.random.uniform(jax.random.fold_in(own, dim), (parts,), jnp.float32, least / len(shards), high / len(shards)))
        level = level * jnp.repeat(draws, shape[dim] // parts).reshape([-1 if axis == dim else 1 for axis in range(len(shape))])
    return level


def centred(key, dims, scale, most, pieces=(), kind=jnp.bfloat16):
    gain = block_levels(key, dims, pieces, -0.22, 0.18) if pieces else 1.0
    result = jax.random.normal(key, dims, jnp.float32) * scale * gain
    return jnp.minimum(jnp.maximum(result, -most), most).astype(kind)


def setup_inputs(seed: int = 0) -> dict:
    splits = jax.random.split(jax.random.key(seed), 6)
    return {
        "signal": centred(splits[0], (SEQUENCE_LENGTH, HEAD_COUNT * P_SIZE), 1.0, 6.0, ((0, 16), (1, 8))),
        "log_decay": draw_log_decay(jax.random.fold_in(splits[5], 71), 0),
        "state_in": centred(splits[2], (SEQUENCE_LENGTH, G * N), 0.025, 0.14941406, ((0, 128),)),
        "state_out": centred(splits[3], (SEQUENCE_LENGTH, G * N), 0.025, 0.14941406, ((0, 128),)),
        "cotangent": centred(splits[4], (SEQUENCE_LENGTH, HEAD_COUNT * P_SIZE), 0.1, 0.59765625, ((0, 16), (1, 8))),
    }


def multiply(pattern, first_op, second_op):
    return jnp.einsum(pattern, first_op.astype(jnp.float32), second_op.astype(jnp.float32))


def masked_exp(chosen, exponent):
    return jnp.where(chosen, jnp.exp(jnp.where(chosen, exponent, 0.0)), 0.0)


def block_mixing(in_rows, out_rows, cumulated):
    positions = jnp.arange(cumulated.shape[0], dtype=jnp.int32)
    below_mask = positions[:, None] >= positions[None, :]
    spread = jnp.transpose(cumulated, (1, 2, 0))
    damping = masked_exp(below_mask, spread[:, :, :, None] - spread[:, :, None, :])
    scores = multiply("tgn,sgn->gts", out_rows, in_rows)
    mixing = (scores[:, None] * damping).astype(jnp.bfloat16)
    return below_mask, damping, mixing


def first_pass(blocks):
    values, grads, in_rows, out_rows, cumulated, block_sum = blocks
    weights_end = jnp.exp(block_sum - cumulated)[..., None]
    weighted = (values.astype(jnp.float32) * weights_end).astype(jnp.bfloat16)
    end_states = multiply("sgjp,sgn->gjpn", weighted, in_rows)
    scaled = (grads.astype(jnp.float32) * jnp.exp(cumulated)[..., None]).astype(jnp.bfloat16)
    direct_adjoint = multiply("tgjp,tgn->gjpn", scaled, out_rows)
    return end_states, direct_adjoint


def finish(values, grads, in_rows, out_rows, cumulated, block_sum, intra_part, below_mask, damping, mixing, start_state, after_adjoint):
    starts_low = start_state.astype(jnp.bfloat16)
    after_low = after_adjoint.astype(jnp.bfloat16)
    weights_start = jnp.exp(cumulated)[..., None]
    weights_end = jnp.exp(block_sum - cumulated)[..., None]
    inter_part = weights_start * multiply("gjpn,tgn->tgjp", starts_low, out_rows)
    output = (intra_part + inter_part).astype(jnp.bfloat16)
    grad_mix = jnp.where(below_mask, multiply("tgjp,sgjp->gjts", grads, values), 0.0)
    grad_scores = jnp.sum(grad_mix * damping, axis=1).astype(jnp.bfloat16)
    back_term = multiply("gjpn,sgn->sgjp", after_low, in_rows)
    grad_values = (multiply("gjts,tgjp->sgjp", mixing, grads) + weights_end * back_term).astype(jnp.bfloat16)
    scaled = (grads.astype(jnp.float32) * weights_start).astype(jnp.bfloat16)
    weighted = (values.astype(jnp.float32) * weights_end).astype(jnp.bfloat16)
    grad_out_rows = (multiply("gts,sgn->tgn", grad_scores, in_rows) + multiply("tgjp,gjpn->tgn", scaled, starts_low)).astype(jnp.bfloat16)
    grad_in_rows = (multiply("gts,tgn->sgn", grad_scores, out_rows) + multiply("sgjp,gjpn->sgn", weighted, after_low)).astype(jnp.bfloat16)
    pair_terms = grad_mix * mixing.astype(jnp.float32)
    weight_grad = jnp.sum(values.astype(jnp.float32) * back_term, axis=-1) * weights_end[..., 0]
    cum_grad = jnp.transpose(jnp.sum(pair_terms, axis=3) - jnp.sum(pair_terms, axis=2), (2, 0, 1))
    cum_grad = cum_grad + jnp.sum(grads.astype(jnp.float32) * inter_part, axis=-1) - weight_grad
    total_grad = jnp.exp(block_sum) * jnp.sum(after_adjoint * start_state, axis=(2, 3)) + jnp.sum(weight_grad, axis=0)
    grad_decay = jnp.flip(jnp.cumsum(jnp.flip(cum_grad, 0), axis=0), 0) + total_grad
    return output, grad_values, grad_in_rows, grad_out_rows, grad_decay


def second_pass(blocks):
    values, grads, in_rows, out_rows, cumulated, block_sum, start_state, after_adjoint = blocks
    below_mask, damping, mixing = block_mixing(in_rows, out_rows, cumulated)
    intra_part = multiply("gjts,sgjp->tgjp", mixing, values)
    return finish(values, grads, in_rows, out_rows, cumulated, block_sum, intra_part, below_mask, damping, mixing, start_state, after_adjoint)


def forward_step(current, element):
    end_state, decay_sum = element
    return jnp.exp(decay_sum)[:, :, None, None] * current + end_state, current


def backward_step(current, element):
    direct_state, decay_sum = element
    return direct_state + jnp.exp(decay_sum)[:, :, None, None] * current, current


def reference(signal, log_decay, state_in, state_out, cotangent):
    length = signal.shape[0]
    block_count = length // Q
    per_group = HEAD_COUNT // G
    signal_blocks = signal.reshape(block_count, Q, G, per_group, P_SIZE)
    grad_blocks = cotangent.reshape(block_count, Q, G, per_group, P_SIZE)
    in_blocks = state_in.reshape(block_count, Q, G, N)
    out_blocks = state_out.reshape(block_count, Q, G, N)
    cum_decay = jnp.cumsum(log_decay.reshape(G, per_group, block_count, Q), axis=-1)
    cum_decay = jnp.transpose(cum_decay, (2, 3, 0, 1))
    block_decay = cum_decay[:, -1]
    end_states, direct_adjoint = lax.map(first_pass, (signal_blocks, grad_blocks, in_blocks, out_blocks, cum_decay, block_decay))
    zero_state = jnp.zeros((G, per_group, P_SIZE, N), jnp.float32)
    _, start_states = lax.scan(forward_step, zero_state, (end_states, block_decay))
    _, after_adjoint = lax.scan(backward_step, zero_state, (direct_adjoint, block_decay), reverse=True)
    results = lax.map(second_pass, (signal_blocks, grad_blocks, in_blocks, out_blocks, cum_decay, block_decay, start_states, after_adjoint))
    output, grad_values, grad_in_rows, grad_out_rows, grad_decay = results
    grad_decay = jnp.transpose(grad_decay, (2, 3, 0, 1)).reshape(HEAD_COUNT, length)
    return (output.reshape(length, HEAD_COUNT * P_SIZE), grad_values.reshape(length, HEAD_COUNT * P_SIZE), grad_in_rows.reshape(length, G * N), grad_out_rows.reshape(length, G * N), grad_decay)
```

```python
import jax
import jax.numpy as jnp
from jax import lax
from jax.experimental import pallas as pl
from jax.experimental.pallas import tpu as pltpu
from jax.sharding import PartitionSpec as P

HEADS = 16
P_SIZE = 64
N = 128
C = 128
LANES = HEADS * P_SIZE
TOKENS = 2048
PIECES = TOKENS // C
ROW = 4
SLICE = LANES // ROW
MIB = 1 << 20

F32 = jnp.float32
BF16 = jnp.bfloat16


def dot(a, b):
    return lax.dot_general(a, b, (((1,), (0,)), ((), ())), preferred_element_type=F32)


def dot_nt(a, b):
    return lax.dot_general(a, b, (((1,), (1,)), ((), ())), preferred_element_type=F32)


def dot_tn(a, b):
    return lax.dot_general(a, b, (((0,), (0,)), ((), ())), preferred_element_type=F32)


def split2(a):
    high = a.astype(BF16)
    return high, (a - high.astype(F32)).astype(BF16)


def split3(a):
    high = a.astype(BF16)
    rest = a - high.astype(F32)
    return (high,) + split2(rest)


def iota(shape, dim):
    return lax.broadcasted_iota(jnp.int32, shape, dim)


def lane_heads(rows):
    return (iota((rows, LANES), 1) // P_SIZE) == (iota((rows, LANES), 0) % HEADS)


def one_hot(chosen):
    return jnp.where(chosen, 1.0, 0.0).astype(BF16)


TILES = 4
TILE = LANES // TILES


def tile(i):
    return slice(i * TILE, (i + 1) * TILE)


def piece_rows(j):
    return pl.ds(pl.multiple_of(j * C, C), C)


def scale_kernel(
    sig_hbm, cot_hbm, ld_ref, us_ref, vs_ref, g_ref, u2_ref, v2_ref, half_ref, ind_ref, sbuf, cbuf, ssem, csem
):
    slots = sbuf.shape[0]

    def reads(j):
        slot = lax.rem(j, slots)
        return (
            pltpu.make_async_copy(sig_hbm.at[piece_rows(j)], sbuf.at[slot], ssem.at[slot]),
            pltpu.make_async_copy(cot_hbm.at[piece_rows(j)], cbuf.at[slot], csem.at[slot]),
        )

    for j in range(slots):
        for copy in reads(j):
            copy.start()

    ind_ref[...] = one_hot(lane_heads(2 * HEADS))
    decay = jnp.concatenate([ld_ref[:, j * C : (j + 1) * C] for j in range(PIECES)], axis=0)
    upto = one_hot(iota((C, C), 0) <= iota((C, C), 1))
    cum = sum(dot(part, upto) for part in split3(decay))
    total = cum[:, C - 1 : C]
    u = jnp.exp(cum - 0.5 * total)
    v = jnp.exp(0.5 * total - cum)
    for ref, value in ((u2_ref, u), (v2_ref, v)):
        high, low = split2(value)
        for j in range(PIECES):
            rows = slice(j * HEADS, (j + 1) * HEADS)
            ref[j] = jnp.concatenate([high[rows], low[rows]], axis=0)
    chosen = lane_heads(HEADS)
    for j in range(PIECES):
        rows = slice(j * HEADS, (j + 1) * HEADS)
        spread = jnp.where(chosen, 0.5 * total[rows], 0.0)
        half_ref[j : j + 1, :] = jnp.sum(spread, axis=0, keepdims=True)

    def piece(j, carry):
        slot = lax.rem(j, slots)
        for copy in reads(j):
            copy.wait()
        u_rows, v_rows = u2_ref[j].T, v2_ref[j].T
        grad = jnp.zeros((C, C), F32)
        for i in range(TILES):
            us = (cbuf[slot, :, tile(i)].astype(F32) * dot(u_rows, ind_ref[:, tile(i)])).astype(BF16)
            vs = (sbuf[slot, :, tile(i)].astype(F32) * dot(v_rows, ind_ref[:, tile(i)])).astype(BF16)
            us_ref[piece_rows(j), tile(i)] = us
            vs_ref[piece_rows(j), tile(i)] = vs
            grad = grad + dot_nt(us, vs)
        g_ref[j] = jnp.where(iota((C, C), 0) >= iota((C, C), 1), grad, 0.0).astype(BF16)

        @pl.when(j + slots < PIECES)
        def _():
            for copy in reads(j + slots):
                copy.start()

        return carry

    lax.fori_loop(0, PIECES, piece, 0)


def log_rows(*logs):
    lanes = logs[0].shape[1]
    place = iota((16, lanes), 0)
    out = jnp.zeros((16, lanes), F32)
    for i, log in enumerate(logs):
        for k, part in enumerate(split3(log)):
            out = jnp.where(place == 3 * i + k, part.astype(F32), out)
    return out


def log_of(block, i=0):
    return jnp.sum(block[3 * i : 3 * i + 3, :], axis=0, keepdims=True)


def scaled(a):
    most = jnp.maximum(jnp.max(jnp.abs(a), axis=0, keepdims=True), 1e-30)
    return a * (1.0 / most), jnp.log(most)


def state_kernel(us_ref, vs_ref, r0, r1, r2, r3, other, half_ref, x_ref, local_ref, after_ref, msg_ref, xt_ref):
    z, core, homes = head_places()
    for d, ref in enumerate((r0, r1, r2, r3)):
        x_ref[2 * homes[d] + core] = ref[core]
        x_ref[2 * homes[d] + 1 - core] = other[d]
    for j in range(PIECES):
        rows = slice((j % 2) * C, (j % 2 + 1) * C)
        for i in range(2):
            xt_ref[i, :, j * C : (j + 1) * C] = x_ref[j // 2, i, rows, :].T
    me = lax.rem(lax.axis_index("ctx"), ROW)

    def part(d, carry):
        lanes = pl.ds(pl.multiple_of(lax.rem(me + d, ROW) * SLICE, SLICE), SLICE)
        state = jnp.zeros((N, SLICE), F32)
        adjoint = jnp.zeros((N, SLICE), F32)
        total = jnp.zeros((1, SLICE), F32)
        for i in range(PIECES):
            k = PIECES - 1 - i
            local_ref[i, :, lanes] = state.astype(BF16)
            half = half_ref[i : i + 1, lanes]
            weight = jnp.exp(half)
            end = dot(xt_ref[0, :, i * C : (i + 1) * C], vs_ref[i * C : (i + 1) * C, lanes])
            state = weight * (weight * state + end)
            total = total + 2.0 * half
            after_ref[k, :, lanes] = adjoint.astype(BF16)
            weight = jnp.exp(half_ref[k : k + 1, lanes])
            end = dot(xt_ref[1, :, k * C : (k + 1) * C], us_ref[k * C : (k + 1) * C, lanes])
            adjoint = weight * (weight * adjoint + end)
        local_ref[PIECES, :, lanes] = state.astype(BF16)
        msg_ref[d, 0:N, :], first = scaled(state)
        msg_ref[d, N : 2 * N, :], second = scaled(adjoint)
        msg_ref[d, 2 * N :, :] = log_rows(total, first, second)
        return carry

    lax.fori_loop(0, ROW, part, 0)


def between(logs, places, chosen):
    total = jnp.zeros_like(logs[0])
    for log, place in zip(logs, places):
        total = total + jnp.where(chosen(place), log, 0.0)
    return total


def pick(flag, log):
    return jnp.where(flag, jnp.exp(log), 0.0)


def head_places():
    index = lax.axis_index("head")
    z, core = lax.div(index, 2), lax.rem(index, 2)
    return z, core, [lax.rem(z + ROW - d, ROW) for d in range(ROW)]


def own_places():
    index = lax.axis_index("ctx")
    x, y = lax.rem(index, ROW), lax.div(index, ROW)
    return x, y, [lax.rem(x + ROW - d, ROW) for d in range(ROW)]


def row_kernel(r0, r1, r2, r3, out_ref):
    x, y, places = own_places()
    refs = (r0, r1, r2, r3)
    ends = [r[2 * N :, :] for r in refs]
    logs = [log_of(end) for end in ends]
    state = jnp.zeros((N, SLICE), F32)
    adjoint = jnp.zeros((N, SLICE), F32)
    for ref, end, own in zip(refs, ends, places):
        state += jnp.exp(between(logs, places, lambda p: p > own) + log_of(end, 1)) * ref[0:N, :]
        adjoint += jnp.exp(between(logs, places, lambda p: p < own) + log_of(end, 2)) * ref[N : 2 * N, :]
    for d in range(1, ROW):
        out_ref[d - 1, 0:N, :], most = scaled(jnp.where(y + d < ROW, state, adjoint))
        out_ref[d - 1, N:, :] = log_rows(sum(logs), most)


def enter_kernel(r0, r1, r2, r3, q1, q2, q3, out_ref):
    x, y, places = own_places()
    refs, rows = (r0, r1, r2, r3), (q1, q2, q3)
    ends = [r[2 * N :, :] for r in refs]
    logs = [log_of(end) for end in ends]
    row_ends = [r[N:, :] for r in rows]
    row_logs = [log_of(end) for end in row_ends]
    row_places = [lax.rem(y + ROW - d, ROW) for d in range(1, ROW)]
    state = jnp.zeros((N, SLICE), F32)
    adjoint = jnp.zeros((N, SLICE), F32)
    for ref, end, own in zip(rows, row_ends, row_places):
        block = ref[0:N, :]
        before = between(row_logs, row_places, lambda p: (p > own) & (p < y)) + log_of(end, 1)
        behind = between(row_logs, row_places, lambda p: (p < own) & (p > y)) + log_of(end, 1)
        state += pick(own < y, before) * block
        adjoint += pick(own > y, behind) * block
    for e in range(ROW):
        to = lax.rem(x + e, ROW)
        first = jnp.exp(between(logs, places, lambda p: p < to)) * state
        second = jnp.exp(between(logs, places, lambda p: p > to)) * adjoint
        for ref, end, own in zip(refs, ends, places):
            before = between(logs, places, lambda p: (p > own) & (p < to)) + log_of(end, 1)
            behind = between(logs, places, lambda p: (p < own) & (p > to)) + log_of(end, 2)
            first += pick(own < to, before) * ref[0:N, :]
            second += pick(own > to, behind) * ref[N : 2 * N, :]
        out_ref[e, 0:N, :], first_log = scaled(first)
        out_ref[e, N : 2 * N, :], second_log = scaled(second)
        out_ref[e, 2 * N :, :] = log_rows(first_log, second_log)


def projection_kernel(
    us_ref,
    vs_ref,
    x_ref,
    g_ref,
    half_ref,
    local_ref,
    after_ref,
    s0,
    s1,
    s2,
    s3,
    grad_ref,
    start_ref,
    behind_ref,
    total_ref,
    enter_ref,
    last_ref,
):
    z, core, homes = head_places()
    x, y, places = own_places()
    for ref, place in zip((s0, s1, s2, s3), places):
        lanes = pl.ds(pl.multiple_of(place * SLICE, SLICE), SLICE)
        end = ref[2 * N :, :]
        enter_ref[0, :, lanes] = jnp.exp(log_of(end, 0)) * ref[0:N, :]
        enter_ref[1, :, lanes] = jnp.exp(log_of(end, 1)) * ref[N : 2 * N, :]
    later = jnp.zeros((1, LANES), F32)
    laters = [None] * PIECES
    for j in reversed(range(PIECES)):
        laters[j] = later
        later = later + 2.0 * half_ref[j : j + 1, :]

    prior = jnp.zeros((1, LANES), F32)
    for j in range(PIECES + 1):
        first = local_ref[j].astype(F32) + jnp.exp(prior) * enter_ref[0]
        if j > 0:
            total_ref[j - 1 : j, :] = jnp.sum(first * last_ref[...], axis=0, keepdims=True)
        if j == PIECES:
            break
        rows = slice(j * C, (j + 1) * C)
        half = half_ref[j : j + 1, :]
        prior = prior + 2.0 * half
        weight = jnp.exp(half)
        part = slice((j % 2) * C, (j % 2 + 1) * C)
        start = (weight * first).astype(BF16)
        start_ref[j] = start
        to = (lax.rem(j // 4 + ROW - z, ROW), j // 2 % 2)
        grad_ref[*to, 1, part, :] = (dot(g_ref[j], x_ref[j // 2, 0, part, :]) + dot_nt(us_ref[rows], start)).astype(BF16)
        second = after_ref[j].astype(F32) + jnp.exp(laters[j]) * enter_ref[1]
        last_ref[...] = second
        behind = (weight * second).astype(BF16)
        behind_ref[j] = behind
        grad_ref[*to, 0, part, :] = (dot_tn(g_ref[j], x_ref[j // 2, 1, part, :]) + dot_nt(vs_ref[rows], behind)).astype(BF16)


def result_kernel(
    us_ref,
    vs_ref,
    start_ref,
    behind_ref,
    x_ref,
    u2_ref,
    v2_ref,
    total_ref,
    out_hbm,
    grad_hbm,
    decay_ref,
    obuf,
    gbuf,
    ind_ref,
    of_ref,
    heads_ref,
    osem,
    gsem,
):
    outs = obuf.shape[0]

    def writes(j):
        slot = lax.rem(j, outs)
        return (
            pltpu.make_async_copy(obuf.at[slot], out_hbm.at[piece_rows(j)], osem.at[slot]),
            pltpu.make_async_copy(gbuf.at[slot], grad_hbm.at[piece_rows(j)], gsem.at[slot]),
        )

    ind_ref[...] = one_hot(lane_heads(2 * HEADS))
    own = ind_ref[0:HEADS, :]
    of_ref[...] = one_hot(iota((LANES, C), 0) // P_SIZE == iota((LANES, C), 1))
    heads_ref[...] = sum(dot_nt(own, part) for part in split3(total_ref[...]))
    lower = iota((C, C), 0) >= iota((C, C), 1)
    upper = iota((C, C), 0) <= iota((C, C), 1)
    from_on = one_hot(lower)

    def piece(j, carry):
        place = lax.rem(j, outs)
        part = pl.ds(pl.multiple_of(lax.rem(j, 2) * C, C), C)
        block = lax.div(j, 2)
        x_in, x_out = x_ref[block, 0, part, :], x_ref[block, 1, part, :]
        scores = jnp.where(lower, dot_nt(x_out, x_in), 0.0).astype(BF16)
        turned = jnp.where(upper, dot_nt(x_in, x_out), 0.0).astype(BF16)
        u_rows, v_rows = u2_ref[j].T, v2_ref[j].T
        left_out = jnp.concatenate([scores, x_out], axis=1)
        left_grad = jnp.concatenate([turned, x_in], axis=1)

        @pl.when(j >= outs)
        def _():
            for copy in writes(j - outs):
                copy.wait()

        total = jnp.sum(jnp.where(iota((HEADS, PIECES), 1) == j, heads_ref[...], 0.0), axis=1, keepdims=True)
        cum_grad = jnp.zeros((C, C), F32)
        for i in range(TILES):
            us, vs = us_ref[piece_rows(j), tile(i)], vs_ref[piece_rows(j), tile(i)]
            out = dot(left_out, jnp.concatenate([vs, start_ref[j, :, tile(i)]], axis=0))
            obuf[place, :, tile(i)] = (out * dot(u_rows, ind_ref[:, tile(i)])).astype(BF16)
            grad = dot(left_grad, jnp.concatenate([us, behind_ref[j, :, tile(i)]], axis=0))
            gbuf[place, :, tile(i)] = (grad * dot(v_rows, ind_ref[:, tile(i)])).astype(BF16)
            diff = us.astype(F32) * out - vs.astype(F32) * grad
            cum_grad = cum_grad + dot(diff.astype(BF16), of_ref[tile(i), :])
        for copy in writes(j):
            copy.start()
        cum_grad = cum_grad.T[0:HEADS] + jnp.where(iota((HEADS, C), 1) == C - 1, total, 0.0)
        sums = dot(jnp.concatenate(split3(cum_grad), axis=0), from_on)
        decay_ref[:, piece_rows(j)] = sums[0:HEADS] + sums[HEADS : 2 * HEADS] + sums[2 * HEADS :]
        return carry

    lax.fori_loop(0, PIECES, piece, 0)
    for j in range(PIECES - outs, PIECES):
        for copy in writes(j):
            copy.wait()


def split_kernel(in_ref, out_ref, *sent):
    z, core, homes = head_places()
    for d, ref in enumerate(sent):
        for to in range(2):
            group = 2 * lax.rem(z + d, ROW) + to
            columns = pl.ds(pl.multiple_of(group * N, N), N)
            ref[to, 0] = in_ref[:, columns]
            ref[to, 1] = out_ref[:, columns]


def swap_kernel(r0, r1, r2, r3, after_hbm, other_ref):
    z, core, homes = head_places()
    for d, ref in enumerate((r0, r1, r2, r3)):
        other_ref[d] = ref[1 - core]


def join_kernel(r0, r1, r2, r3, other, in_ref, out_ref):
    z, core, homes = head_places()
    for d, ref in enumerate((r0, r1, r2, r3)):
        columns = pl.ds(pl.multiple_of((2 * homes[d] + core) * N, N), N)
        in_ref[:, columns] = ref[core, 0]
        out_ref[:, columns] = ref[core, 1]
        columns = pl.ds(pl.multiple_of((2 * homes[d] + 1 - core) * N, N), N)
        in_ref[:, columns] = other[d, 0]
        out_ref[:, columns] = other[d, 1]


VMEM = pl.BlockSpec(memory_space=pltpu.VMEM)
HBM = pl.BlockSpec(memory_space=pltpu.HBM)
DMA = pltpu.SemaphoreType.DMA


def call(kernel, args, outs, specs, out_specs, scratch=(), limit=10, flops=0, moved=0):
    return pl.pallas_call(
        kernel,
        out_shape=outs,
        in_specs=specs,
        out_specs=out_specs,
        scratch_shapes=list(scratch),
        compiler_params=pltpu.CompilerParams(vmem_limit_bytes=limit * MIB),
        cost_estimate=pl.CostEstimate(flops=flops, bytes_accessed=moved, transcendentals=0),
    )(*args)


def held(shape, dtype=BF16):
    return pltpu.VMEM(shape, dtype)


def far(a):
    return pltpu.with_memory_space_constraint(a, pltpu.HBM)


def kept(shape, dtype=BF16):
    return pltpu.HBM(shape, dtype)


def plain(shape, dtype=BF16):
    return jax.ShapeDtypeStruct(shape, dtype)


def along_x(d):
    return [(y * ROW + x, y * ROW + (x + d) % ROW) for y in range(ROW) for x in range(ROW)]


def along_y(d):
    return [(y * ROW + x, (y + d) % ROW * ROW + x) for y in range(ROW) for x in range(ROW)]


def along_z(d):
    return [(z * 2 + c, (z + d) % ROW * 2 + c) for z in range(ROW) for c in range(2)]


def send(a, pairs):
    return lax.ppermute(a.astype(jnp.float16), "ctx", pairs).astype(F32)


OTHER_CORE = [(i, i ^ 1) for i in range(2 * ROW)]


def body(signal, log_decay, state_in, state_out, cotangent):
    own = state_in.shape[0]
    chip = (2, 2, own, N)
    blocks = (2 * ROW, 2, own, N)
    wide = (TOKENS, LANES)
    states = (PIECES, N, LANES)
    band = (C, LANES)

    sent = call(split_kernel, (state_in, state_out), [held(chip)] * ROW, [VMEM] * 2, [VMEM] * ROW)
    got = [sent[0]] + [lax.ppermute(sent[d], "head", along_z(d)) for d in (1, 3, 2)]
    got = [got[0], got[1], got[3], got[2]]
    us, vs, g, u2, v2, half = call(
        scale_kernel,
        (far(signal), far(cotangent), log_decay),
        (
            held(wide),
            held(wide),
            held((PIECES, C, C)),
            held((PIECES, 2 * HEADS, C)),
            held((PIECES, 2 * HEADS, C)),
            held((PIECES, LANES), F32),
        ),
        [HBM, HBM, VMEM],
        [VMEM] * 6,
        [pltpu.VMEM((2 * HEADS, LANES), BF16)] + [pltpu.VMEM((4,) + band, BF16)] * 2 + [DMA((4,))] * 2,
        flops=1 << 33,
        moved=1 << 23,
    )
    other = call(swap_kernel, got + [half], held((ROW, 2, own, N)), [VMEM] * 5, VMEM)
    other = lax.ppermute(other, "head", OTHER_CORE)
    x, local, after, msg = call(
        state_kernel,
        [us, vs] + got + [other, half],
        (held(blocks), held((PIECES + 1, N, LANES)), held(states), held((ROW, 2 * N + 16, SLICE), F32)),
        [VMEM] * 8,
        [VMEM] * 4,
        [pltpu.VMEM((2, N, TOKENS), BF16)],
    )
    mates = [msg[0]] + [send(msg[d], along_x(d)) for d in range(1, ROW)]
    totals = call(row_kernel, mates, held((ROW - 1, N + 16, SLICE), F32), [VMEM] * 4, VMEM)
    rows = [send(totals[d - 1], along_y(d)) for d in range(1, ROW)]
    back = call(enter_kernel, mates + rows, held((ROW, 2 * N + 16, SLICE), F32), [VMEM] * 7, VMEM)
    shares = [back[0]] + [send(back[e], along_x(e)) for e in range(1, ROW)]
    grads, start, behind, total = call(
        projection_kernel,
        [us, vs, x, g, half, local, after] + shares,
        (held((ROW,) + chip), held(states), held(states), held((PIECES, LANES), F32)),
        [VMEM] * 11,
        [VMEM] * 4,
        [pltpu.VMEM((2,) + band, F32), pltpu.VMEM(band, F32)],
    )
    returned = [grads[0]] + [lax.ppermute(grads[d], "head", along_z(d)) for d in (1, 3, 2)]
    returned = [returned[0], returned[1], returned[3], returned[2]]
    output, grad_signal, grad_decay = call(
        result_kernel,
        (us, vs, start, behind, x, u2, v2, total),
        (plain(wide), plain(wide), plain((HEADS, TOKENS), F32)),
        [VMEM] * 8,
        [HBM, HBM, VMEM],
        [pltpu.VMEM((2,) + band, BF16)] * 2
        + [pltpu.VMEM((2 * HEADS, LANES), BF16), pltpu.VMEM((LANES, C), BF16), pltpu.VMEM((HEADS, PIECES), F32)]
        + [DMA((2,)), DMA((2,))],
        flops=1 << 34,
        moved=1 << 23,
    )
    other = call(swap_kernel, returned + [far(grad_decay)], held((ROW, 2, own, N)), [VMEM] * ROW + [HBM], VMEM)
    other = lax.ppermute(other, "head", OTHER_CORE)
    narrow = plain(state_in.shape)
    grad_in, grad_out = call(join_kernel, returned + [other], (narrow, narrow), [VMEM] * 5, [VMEM] * 2)
    return output, grad_signal, grad_in, grad_out, grad_decay


def solution(mesh):
    in_specs = (
        P("ctx", "head"),
        P("head", "ctx"),
        P(("ctx", "head"), None),
        P(("ctx", "head"), None),
        P("ctx", "head"),
    )
    out_specs = (
        P("ctx", "head"),
        P("ctx", "head"),
        P(("ctx", "head"), None),
        P(("ctx", "head"), None),
        P("head", "ctx"),
    )
    return jax.shard_map(body, mesh=mesh, in_specs=in_specs, out_specs=out_specs, check_vma=False)
```

```python
import jax
import jax.numpy as jnp
from jax import lax
from jax.experimental import pallas as pl
from jax.experimental.pallas import tpu as pltpu
from jax.sharding import PartitionSpec as P

HEADS = 16
P_SIZE = 64
N = 128
C = 128
LANES = HEADS * P_SIZE
TOKENS = 2048
PIECES = TOKENS // C
ROW = 4
SLICE = LANES // ROW
MIB = 1 << 20

F32 = jnp.float32
BF16 = jnp.bfloat16


def dot(a, b):
    return lax.dot_general(a, b, (((1,), (0,)), ((), ())), preferred_element_type=F32)


def dot_nt(a, b):
    return lax.dot_general(a, b, (((1,), (1,)), ((), ())), preferred_element_type=F32)


def dot_tn(a, b):
    return lax.dot_general(a, b, (((0,), (0,)), ((), ())), preferred_element_type=F32)


def split2(a):
    high = a.astype(BF16)
    return high, (a - high.astype(F32)).astype(BF16)


def split3(a):
    high = a.astype(BF16)
    rest = a - high.astype(F32)
    return (high,) + split2(rest)


def iota(shape, dim):
    return lax.broadcasted_iota(jnp.int32, shape, dim)


def lane_heads(rows):
    return (iota((rows, LANES), 1) // P_SIZE) == (iota((rows, LANES), 0) % HEADS)


def one_hot(chosen):
    return jnp.where(chosen, 1.0, 0.0).astype(BF16)


TILES = 4
TILE = LANES // TILES


def tile(i):
    return slice(i * TILE, (i + 1) * TILE)


def piece_rows(j):
    return pl.ds(pl.multiple_of(j * C, C), C)


def scale_kernel(
    sig_hbm, cot_hbm, ld_ref, us_ref, vs_ref, u2_ref, v2_ref, half_ref, ind_ref, sbuf, cbuf, ssem, csem
):
    slots = sbuf.shape[0]

    def reads(j):
        slot = lax.rem(j, slots)
        return (
            pltpu.make_async_copy(sig_hbm.at[piece_rows(j)], sbuf.at[slot], ssem.at[slot]),
            pltpu.make_async_copy(cot_hbm.at[piece_rows(j)], cbuf.at[slot], csem.at[slot]),
        )

    for j in range(slots):
        for copy in reads(j):
            copy.start()

    ind_ref[...] = one_hot(lane_heads(2 * HEADS))
    decay = jnp.concatenate([ld_ref[:, j * C : (j + 1) * C] for j in range(PIECES)], axis=0)
    upto = one_hot(iota((C, C), 0) <= iota((C, C), 1))
    cum = sum(dot(part, upto) for part in split3(decay))
    total = cum[:, C - 1 : C]
    u = jnp.exp(cum - 0.5 * total)
    v = jnp.exp(0.5 * total - cum)
    for ref, value in ((u2_ref, u), (v2_ref, v)):
        high, low = split2(value)
        for j in range(PIECES):
            rows = slice(j * HEADS, (j + 1) * HEADS)
            ref[j] = jnp.concatenate([high[rows], low[rows]], axis=0)
    chosen = lane_heads(HEADS)
    for j in range(PIECES):
        rows = slice(j * HEADS, (j + 1) * HEADS)
        spread = jnp.where(chosen, 0.5 * total[rows], 0.0)
        half_ref[j : j + 1, :] = jnp.sum(spread, axis=0, keepdims=True)

    def piece(j, carry):
        slot = lax.rem(j, slots)
        for copy in reads(j):
            copy.wait()
        u_rows, v_rows = u2_ref[j].T, v2_ref[j].T
        for i in range(TILES):
            us = (cbuf[slot, :, tile(i)].astype(F32) * dot(u_rows, ind_ref[:, tile(i)])).astype(BF16)
            vs = (sbuf[slot, :, tile(i)].astype(F32) * dot(v_rows, ind_ref[:, tile(i)])).astype(BF16)
            us_ref[piece_rows(j), tile(i)] = us
            vs_ref[piece_rows(j), tile(i)] = vs

        @pl.when(j + slots < PIECES)
        def _():
            for copy in reads(j + slots):
                copy.start()

        return carry

    lax.fori_loop(0, PIECES, piece, 0)


def log_rows(*logs):
    lanes = logs[0].shape[1]
    place = iota((16, lanes), 0)
    out = jnp.zeros((16, lanes), F32)
    for i, log in enumerate(logs):
        for k, part in enumerate(split3(log)):
            out = jnp.where(place == 3 * i + k, part.astype(F32), out)
    return out


def log_of(block, i=0):
    return jnp.sum(block[3 * i : 3 * i + 3, :], axis=0, keepdims=True)


def scaled(a):
    most = jnp.maximum(jnp.max(jnp.abs(a), axis=0, keepdims=True), 1e-30)
    return a * (1.0 / most), jnp.log(most)


def state_part(d, us_ref, vs_ref, xt_ref, half_ref, local_ref, after_ref, msg_ref):
    me = lax.rem(lax.axis_index("ctx"), ROW)
    lanes = pl.ds(pl.multiple_of(lax.rem(me + d, ROW) * SLICE, SLICE), SLICE)
    state = jnp.zeros((N, SLICE), F32)
    adjoint = jnp.zeros((N, SLICE), F32)
    total = jnp.zeros((1, SLICE), F32)
    for i in range(PIECES):
        k = PIECES - 1 - i
        local_ref[i, :, lanes] = state.astype(BF16)
        half = half_ref[i : i + 1, lanes]
        weight = jnp.exp(half)
        end = dot(xt_ref[0, :, i * C : (i + 1) * C], vs_ref[i * C : (i + 1) * C, lanes])
        state = weight * (weight * state + end)
        total = total + 2.0 * half
        after_ref[k, :, lanes] = adjoint.astype(BF16)
        weight = jnp.exp(half_ref[k : k + 1, lanes])
        end = dot(xt_ref[1, :, k * C : (k + 1) * C], us_ref[k * C : (k + 1) * C, lanes])
        adjoint = weight * (weight * adjoint + end)
    local_ref[PIECES, :, lanes] = state.astype(BF16)
    msg_ref[0:N, :], first = scaled(state)
    msg_ref[N : 2 * N, :], second = scaled(adjoint)
    msg_ref[2 * N :, :] = log_rows(total, first, second)


def state_kernel(us_ref, vs_ref, r0, r1, r2, r3, other, half_ref, x_ref, xt_ref, local_ref, after_ref, msg_ref):
    z, core, homes = head_places()
    for d, ref in enumerate((r0, r1, r2, r3)):
        x_ref[2 * homes[d] + core] = ref[core]
        x_ref[2 * homes[d] + 1 - core] = other[d]
    for j in range(PIECES):
        rows = slice((j % 2) * C, (j % 2 + 1) * C)
        for i in range(2):
            xt_ref[i, :, j * C : (j + 1) * C] = x_ref[j // 2, i, rows, :].T

    def part(d, carry):
        state_part(d, us_ref, vs_ref, xt_ref, half_ref, local_ref, after_ref, msg_ref.at[d - 1])
        return carry

    lax.fori_loop(1, ROW, part, 0)


def own_state_kernel(us_ref, vs_ref, xt_ref, half_ref, local_in, after_in, local_ref, after_ref, msg_ref):
    state_part(0, us_ref, vs_ref, xt_ref, half_ref, local_ref, after_ref, msg_ref)


def between(logs, places, chosen):
    total = jnp.zeros_like(logs[0])
    for log, place in zip(logs, places):
        total = total + jnp.where(chosen(place), log, 0.0)
    return total


def pick(flag, log):
    return jnp.where(flag, jnp.exp(log), 0.0)


def intra_kernel(us_ref, vs_ref, x_ref, after_ref, base_ref, of_ref):
    of_ref[...] = one_hot(iota((LANES, C), 0) // P_SIZE == iota((LANES, C), 1))
    lower = iota((C, C), 0) >= iota((C, C), 1)

    def piece(j, carry):
        rows = piece_rows(j)
        part = pl.ds(pl.multiple_of(lax.rem(j, 2) * C, C), C)
        block = lax.div(j, 2)
        grad = jnp.where(lower, dot_nt(us_ref[rows, :], vs_ref[rows, :]), 0.0).astype(BF16)
        base_ref[j, 0] = dot_tn(grad, x_ref[block, 1, part, :])
        base_ref[j, 1] = dot(grad, x_ref[block, 0, part, :])
        return carry

    lax.fori_loop(0, PIECES, piece, 0, unroll=2)


def head_places():
    index = lax.axis_index("head")
    z, core = lax.div(index, 2), lax.rem(index, 2)
    return z, core, [lax.rem(z + ROW - d, ROW) for d in range(ROW)]


def own_places():
    index = lax.axis_index("ctx")
    x, y = lax.rem(index, ROW), lax.div(index, ROW)
    return x, y, [lax.rem(x + ROW - d, ROW) for d in range(ROW)]


def row_kernel(r0, r1, r2, r3, base_ref, out_ref):
    x, y, places = own_places()
    refs = (r0, r1, r2, r3)
    ends = [r[2 * N :, :] for r in refs]
    logs = [log_of(end) for end in ends]
    state = jnp.zeros((N, SLICE), F32)
    adjoint = jnp.zeros((N, SLICE), F32)
    for ref, end, own in zip(refs, ends, places):
        state += jnp.exp(between(logs, places, lambda p: p > own) + log_of(end, 1)) * ref[0:N, :]
        adjoint += jnp.exp(between(logs, places, lambda p: p < own) + log_of(end, 2)) * ref[N : 2 * N, :]
    for d in range(1, ROW):
        out_ref[d - 1, 0:N, :], most = scaled(jnp.where(y + d < ROW, state, adjoint))
        out_ref[d - 1, N:, :] = log_rows(sum(logs), most)


def enter_kernel(r0, r1, r2, r3, q1, q2, q3, out_ref):
    x, y, places = own_places()
    refs, rows = (r0, r1, r2, r3), (q1, q2, q3)
    ends = [r[2 * N :, :] for r in refs]
    logs = [log_of(end) for end in ends]
    row_ends = [r[N:, :] for r in rows]
    row_logs = [log_of(end) for end in row_ends]
    row_places = [lax.rem(y + ROW - d, ROW) for d in range(1, ROW)]
    state = jnp.zeros((N, SLICE), F32)
    adjoint = jnp.zeros((N, SLICE), F32)
    for ref, end, own in zip(rows, row_ends, row_places):
        block = ref[0:N, :]
        before = between(row_logs, row_places, lambda p: (p > own) & (p < y)) + log_of(end, 1)
        behind = between(row_logs, row_places, lambda p: (p < own) & (p > y)) + log_of(end, 1)
        state += pick(own < y, before) * block
        adjoint += pick(own > y, behind) * block
    for e in range(ROW):
        to = lax.rem(x + e, ROW)
        first = jnp.exp(between(logs, places, lambda p: p < to)) * state
        second = jnp.exp(between(logs, places, lambda p: p > to)) * adjoint
        for ref, end, own in zip(refs, ends, places):
            before = between(logs, places, lambda p: (p > own) & (p < to)) + log_of(end, 1)
            behind = between(logs, places, lambda p: (p < own) & (p > to)) + log_of(end, 2)
            first += pick(own < to, before) * ref[0:N, :]
            second += pick(own > to, behind) * ref[N : 2 * N, :]
        out_ref[e, 0:N, :], first_log = scaled(first)
        out_ref[e, N : 2 * N, :], second_log = scaled(second)
        out_ref[e, 2 * N :, :] = log_rows(first_log, second_log)


def projection_kernel(
    us_ref,
    vs_ref,
    base_ref,
    half_ref,
    local_ref,
    after_ref,
    s0,
    s1,
    s2,
    s3,
    grad_ref,
    start_ref,
    behind_ref,
    total_ref,
    enter_ref,
    last_ref,
):
    z, core, homes = head_places()
    x, y, places = own_places()
    for ref, place in zip((s0, s1, s2, s3), places):
        lanes = pl.ds(pl.multiple_of(place * SLICE, SLICE), SLICE)
        end = ref[2 * N :, :]
        enter_ref[0, :, lanes] = jnp.exp(log_of(end, 0)) * ref[0:N, :]
        enter_ref[1, :, lanes] = jnp.exp(log_of(end, 1)) * ref[N : 2 * N, :]
    later = jnp.zeros((1, LANES), F32)
    laters = [None] * PIECES
    for j in reversed(range(PIECES)):
        laters[j] = later
        later = later + 2.0 * half_ref[j : j + 1, :]

    prior = jnp.zeros((1, LANES), F32)
    for j in range(PIECES + 1):
        before = jnp.exp(prior)
        if j < PIECES:
            rows = slice(j * C, (j + 1) * C)
            half = half_ref[j : j + 1, :]
            prior = prior + 2.0 * half
            weight, later = jnp.exp(half), jnp.exp(laters[j])
            part = slice((j % 2) * C, (j % 2 + 1) * C)
            to = (lax.rem(j // 4 + ROW - z, ROW), j // 2 % 2)
            grad_out, grad_in = base_ref[j, 1], base_ref[j, 0]
        for i in range(TILES):
            t = tile(i)
            first = local_ref[j, :, t].astype(F32) + before[:, t] * enter_ref[0, :, t]
            if j > 0:
                total_ref[j - 1 : j, t] = jnp.sum(first * last_ref[:, t], axis=0, keepdims=True)
            if j == PIECES:
                continue
            start = (weight[:, t] * first).astype(BF16)
            start_ref[j, :, t] = start
            grad_out = grad_out + dot_nt(us_ref[rows, t], start)
            second = after_ref[j, :, t].astype(F32) + later[:, t] * enter_ref[1, :, t]
            last_ref[:, t] = second
            behind = (weight[:, t] * second).astype(BF16)
            behind_ref[j, :, t] = behind
            grad_in = grad_in + dot_nt(vs_ref[rows, t], behind)
        if j < PIECES:
            grad_ref[*to, 1, part, :] = grad_out.astype(BF16)
            grad_ref[*to, 0, part, :] = grad_in.astype(BF16)


def result_kernel(
    us_ref,
    vs_ref,
    start_ref,
    behind_ref,
    x_ref,
    u2_ref,
    v2_ref,
    out_hbm,
    grad_hbm,
    diff_ref,
    obuf,
    gbuf,
    ind_ref,
    osem,
    gsem,
):
    outs = obuf.shape[0]

    def writes(j):
        slot = lax.rem(j, outs)
        return (
            pltpu.make_async_copy(obuf.at[slot], out_hbm.at[piece_rows(j)], osem.at[slot]),
            pltpu.make_async_copy(gbuf.at[slot], grad_hbm.at[piece_rows(j)], gsem.at[slot]),
        )

    ind_ref[...] = one_hot(lane_heads(2 * HEADS))
    lower = iota((C, C), 0) >= iota((C, C), 1)
    upper = iota((C, C), 0) <= iota((C, C), 1)

    def piece(j, carry):
        place = lax.rem(j, outs)
        part = pl.ds(pl.multiple_of(lax.rem(j, 2) * C, C), C)
        block = lax.div(j, 2)
        x_in, x_out = x_ref[block, 0, part, :], x_ref[block, 1, part, :]
        scores = jnp.where(lower, dot_nt(x_out, x_in), 0.0).astype(BF16)
        turned = jnp.where(upper, dot_nt(x_in, x_out), 0.0).astype(BF16)
        u_rows, v_rows = u2_ref[j].T, v2_ref[j].T
        left_out = jnp.concatenate([scores, x_out], axis=1)
        left_grad = jnp.concatenate([turned, x_in], axis=1)

        @pl.when(j >= outs)
        def _():
            for copy in writes(j - outs):
                copy.wait()

        for i in range(TILES):
            us, vs = us_ref[piece_rows(j), tile(i)], vs_ref[piece_rows(j), tile(i)]
            out = dot(left_out, jnp.concatenate([vs, start_ref[j, :, tile(i)]], axis=0))
            obuf[place, :, tile(i)] = (out * dot(u_rows, ind_ref[:, tile(i)])).astype(BF16)
            grad = dot(left_grad, jnp.concatenate([us, behind_ref[j, :, tile(i)]], axis=0))
            gbuf[place, :, tile(i)] = (grad * dot(v_rows, ind_ref[:, tile(i)])).astype(BF16)
            diff = us.astype(F32) * out - vs.astype(F32) * grad
            diff_ref[piece_rows(j), tile(i)] = diff.astype(BF16)
        for copy in writes(j):
            copy.start()
        return carry

    lax.fori_loop(0, PIECES, piece, 0, unroll=2)
    for j in range(PIECES - outs, PIECES):
        for copy in writes(j):
            copy.wait()


def decay_part(k, diff_ref, total_ref, of_ref, decay_ref):
    own = one_hot(lane_heads(HEADS))
    from_on = one_hot(iota((C, C), 0) >= iota((C, C), 1))
    last = iota((HEADS, C), 1) == C - 1
    totals = sum(dot_nt(own, part) for part in split3(total_ref[...]))
    cum_grad = dot(diff_ref[4 * k * C : 4 * (k + 1) * C, :], of_ref[...])
    parts = []
    for j in range(4):
        total = totals[:, 4 * k + j : 4 * k + j + 1]
        parts.append(cum_grad[j * C : (j + 1) * C].T[0:HEADS] + jnp.where(last, total, 0.0))
    sums = sum(dot(part, from_on) for part in split3(jnp.concatenate(parts, axis=0)))
    for j in range(4):
        decay_ref[:, (4 * k + j) * C : (4 * k + j + 1) * C] = sums[j * HEADS : (j + 1) * HEADS]


def first_decay_kernel(diff_ref, total_ref, of_ref, decay_ref):
    for k in range(2):
        decay_part(k, diff_ref, total_ref, of_ref, decay_ref)


def decay_kernel(diff_ref, total_ref, of_ref, first_ref, decay_ref):
    decay_ref[:, 0 : TOKENS // 2] = first_ref[...]
    for k in range(2, 4):
        decay_part(k, diff_ref, total_ref, of_ref, decay_ref)


def split_kernel(in_hbm, out_hbm, s0, s1, s2, s3, sems):
    z, core, homes = head_places()
    copies = []
    for d, ref in enumerate((s0, s1, s2, s3)):
        for to in range(2):
            group = 2 * lax.rem(z + d, ROW) + to
            columns = pl.ds(pl.multiple_of(group * N, N), N)
            for i, source in enumerate((in_hbm, out_hbm)):
                copies.append(pltpu.make_async_copy(source.at[:, columns], ref.at[to, i], sems.at[d, to, i]))
    for copy in copies:
        copy.start()
    for copy in copies:
        copy.wait()


def swap_kernel(r0, r1, r2, r3, after_hbm, other_ref):
    z, core, homes = head_places()
    for d, ref in enumerate((r0, r1, r2, r3)):
        other_ref[d] = ref[1 - core]


def join_kernel(r0, r1, r2, r3, other, after_hbm, in_ref, out_ref):
    z, core, homes = head_places()
    for d, ref in enumerate((r0, r1, r2, r3)):
        columns = pl.ds(pl.multiple_of((2 * homes[d] + core) * N, N), N)
        in_ref[:, columns] = ref[core, 0]
        out_ref[:, columns] = ref[core, 1]
        columns = pl.ds(pl.multiple_of((2 * homes[d] + 1 - core) * N, N), N)
        in_ref[:, columns] = other[d, 0]
        out_ref[:, columns] = other[d, 1]


VMEM = pl.BlockSpec(memory_space=pltpu.VMEM)
HBM = pl.BlockSpec(memory_space=pltpu.HBM)
DMA = pltpu.SemaphoreType.DMA


def call(kernel, args, outs, specs, out_specs, scratch=(), limit=10, flops=0, moved=0, aliases={}):
    return pl.pallas_call(
        kernel,
        out_shape=outs,
        in_specs=specs,
        out_specs=out_specs,
        scratch_shapes=list(scratch),
        input_output_aliases=aliases,
        compiler_params=pltpu.CompilerParams(vmem_limit_bytes=limit * MIB),
        cost_estimate=pl.CostEstimate(flops=flops, bytes_accessed=moved, transcendentals=0),
    )(*args)


def held(shape, dtype=BF16):
    return pltpu.VMEM(shape, dtype)


def far(a):
    return pltpu.with_memory_space_constraint(a, pltpu.HBM)


def kept(shape, dtype=BF16):
    return pltpu.HBM(shape, dtype)


def plain(shape, dtype=BF16):
    return jax.ShapeDtypeStruct(shape, dtype)


def along_x(d):
    return [(y * ROW + x, y * ROW + (x + d) % ROW) for y in range(ROW) for x in range(ROW)]


def along_y(d):
    return [(y * ROW + x, (y + d) % ROW * ROW + x) for y in range(ROW) for x in range(ROW)]


def along_z(d):
    return [(z * 2 + c, (z + d) % ROW * 2 + c) for z in range(ROW) for c in range(2)]


def send(a, pairs):
    return lax.ppermute(a.astype(jnp.float16), "ctx", pairs).astype(F32)


OTHER_CORE = [(i, i ^ 1) for i in range(2 * ROW)]


def body(signal, log_decay, state_in, state_out, cotangent):
    own = state_in.shape[0]
    chip = (2, 2, own, N)
    blocks = (2 * ROW, 2, own, N)
    wide = (TOKENS, LANES)
    states = (PIECES, N, LANES)
    band = (C, LANES)

    sent = call(
        split_kernel, (far(state_in), far(state_out)), [held(chip)] * ROW, [HBM] * 2, [VMEM] * ROW, [DMA((ROW, 2, 2))]
    )
    got = [sent[0]] + [lax.ppermute(sent[d], "head", along_z(d)) for d in (1, 3, 2)]
    got = [got[0], got[1], got[3], got[2]]
    us, vs, u2, v2, half = call(
        scale_kernel,
        (far(signal), far(cotangent), log_decay),
        (
            held(wide),
            held(wide),
            held((PIECES, 2 * HEADS, C)),
            held((PIECES, 2 * HEADS, C)),
            held((PIECES, LANES), F32),
        ),
        [HBM, HBM, VMEM],
        [VMEM] * 5,
        [pltpu.VMEM((2 * HEADS, LANES), BF16)] + [pltpu.VMEM((4,) + band, BF16)] * 2 + [DMA((4,))] * 2,
        flops=1 << 33,
        moved=1 << 23,
    )
    other = call(swap_kernel, got + [half], held((ROW, 2, own, N)), [VMEM] * 5, VMEM)
    other = lax.ppermute(other, "head", OTHER_CORE)
    x, xt, local, after, msg = call(
        state_kernel,
        [us, vs] + got + [other, half],
        (
            held(blocks),
            held((2, N, TOKENS)),
            held((PIECES + 1, N, LANES)),
            held(states),
            held((ROW - 1, 2 * N + 16, SLICE), F32),
        ),
        [VMEM] * 8,
        [VMEM] * 5,
    )
    mates = [send(msg[d - 1], along_x(d)) for d in range(1, ROW)]
    local, after, own_msg = call(
        own_state_kernel,
        (us, vs, xt, half, local, after),
        (held((PIECES + 1, N, LANES)), held(states), held((2 * N + 16, SLICE), F32)),
        [VMEM] * 6,
        [VMEM] * 3,
        aliases={4: 0, 5: 1},
        flops=1 << 31,
        moved=1 << 23,
    )
    mates = [own_msg] + mates
    base, of_head = call(
        intra_kernel,
        (us, vs, x, local),
        (held((PIECES, 2, C, N), F32), held((LANES, C))),
        [VMEM] * 4,
        [VMEM] * 2,
        flops=1 << 33,
        moved=1 << 23,
    )
    totals = call(row_kernel, mates + [base], held((ROW - 1, N + 16, SLICE), F32), [VMEM] * 5, VMEM)
    rows = [send(totals[d - 1], along_y(d)) for d in range(1, ROW)]
    back = call(enter_kernel, mates + rows, held((ROW, 2 * N + 16, SLICE), F32), [VMEM] * 7, VMEM)
    shares = [back[0]] + [send(back[e], along_x(e)) for e in range(1, ROW)]
    grads, start, behind, total = call(
        projection_kernel,
        [us, vs, base, half, local, after] + shares,
        (held((ROW,) + chip), held(states), held(states), held((PIECES, LANES), F32)),
        [VMEM] * 10,
        [VMEM] * 4,
        [pltpu.VMEM((2,) + band, F32), pltpu.VMEM(band, F32)],
    )
    returned = [grads[0]] + [lax.ppermute(grads[d], "head", along_z(d)) for d in (1, 3, 2)]
    returned = [returned[0], returned[1], returned[3], returned[2]]
    output, grad_signal, diff = call(
        result_kernel,
        (us, vs, start, behind, x, u2, v2),
        (plain(wide), plain(wide), held(wide)),
        [VMEM] * 7,
        [HBM, HBM, VMEM],
        [pltpu.VMEM((4,) + band, BF16)] * 2 + [pltpu.VMEM((2 * HEADS, LANES), BF16), DMA((4,)), DMA((4,))],
        flops=1 << 34,
        moved=1 << 23,
    )
    decay = call(first_decay_kernel, (diff, total, of_head), held((HEADS, TOKENS // 2), F32), [VMEM] * 3, VMEM)
    other = call(swap_kernel, returned + [decay], held((ROW, 2, own, N)), [VMEM] * 5, VMEM)
    other = lax.ppermute(other, "head", OTHER_CORE)
    grad_decay = call(
        decay_kernel, (diff, total, of_head, decay), plain((HEADS, TOKENS), F32), [VMEM] * 4, VMEM, flops=1 << 31, moved=1 << 22
    )
    narrow = plain(state_in.shape)
    grad_in, grad_out = call(
        join_kernel, returned + [other, far(grad_decay)], (narrow, narrow), [VMEM] * 5 + [HBM], [VMEM] * 2
    )
    return output, grad_signal, grad_in, grad_out, grad_decay


def solution(mesh):
    in_specs = (
        P("ctx", "head"),
        P("head", "ctx"),
        P(("ctx", "head"), None),
        P(("ctx", "head"), None),
        P("ctx", "head"),
    )
    out_specs = (
        P("ctx", "head"),
        P("ctx", "head"),
        P(("ctx", "head"), None),
        P(("ctx", "head"), None),
        P("head", "ctx"),
    )
    return jax.shard_map(body, mesh=mesh, in_specs=in_specs, out_specs=out_specs, check_vma=False)
```

```python
import jax
import jax.numpy as jnp
from jax import lax
from jax.experimental import pallas as pl
from jax.experimental.pallas import tpu as pltpu
from jax.sharding import PartitionSpec as P

HEADS = 16
P_SIZE = 64
N = 128
C = 128
LANES = HEADS * P_SIZE
TOKENS = 2048
PIECES = TOKENS // C
ROW = 4
SLICE = LANES // ROW
MIB = 1 << 20

F32 = jnp.float32
BF16 = jnp.bfloat16


def dot(a, b):
    return lax.dot_general(a, b, (((1,), (0,)), ((), ())), preferred_element_type=F32)


def dot_nt(a, b):
    return lax.dot_general(a, b, (((1,), (1,)), ((), ())), preferred_element_type=F32)


def dot_tn(a, b):
    return lax.dot_general(a, b, (((0,), (0,)), ((), ())), preferred_element_type=F32)


def split2(a):
    high = a.astype(BF16)
    return high, (a - high.astype(F32)).astype(BF16)


def split3(a):
    high = a.astype(BF16)
    rest = a - high.astype(F32)
    return (high,) + split2(rest)


def iota(shape, dim):
    return lax.broadcasted_iota(jnp.int32, shape, dim)


def lane_heads(rows):
    return (iota((rows, LANES), 1) // P_SIZE) == (iota((rows, LANES), 0) % HEADS)


def one_hot(chosen):
    return jnp.where(chosen, 1.0, 0.0).astype(BF16)


TILES = 4
TILE = LANES // TILES


def tile(i):
    return slice(i * TILE, (i + 1) * TILE)


def piece_rows(j):
    return pl.ds(pl.multiple_of(j * C, C), C)


def scale_kernel(
    sig_hbm, cot_hbm, ld_ref, us_ref, vs_ref, u2_ref, v2_ref, half_ref, ind_ref, sbuf, cbuf, ssem, csem
):
    slots = sbuf.shape[0]

    def reads(j):
        slot = lax.rem(j, slots)
        return (
            pltpu.make_async_copy(sig_hbm.at[piece_rows(j)], sbuf.at[slot], ssem.at[slot]),
            pltpu.make_async_copy(cot_hbm.at[piece_rows(j)], cbuf.at[slot], csem.at[slot]),
        )

    for j in range(slots):
        for copy in reads(j):
            copy.start()

    ind_ref[...] = one_hot(lane_heads(2 * HEADS))
    decay = jnp.concatenate([ld_ref[:, j * C : (j + 1) * C] for j in range(PIECES)], axis=0)
    upto = one_hot(iota((C, C), 0) <= iota((C, C), 1))
    cum = sum(dot(part, upto) for part in split3(decay))
    total = cum[:, C - 1 : C]
    u = jnp.exp(cum - 0.5 * total)
    v = jnp.exp(0.5 * total - cum)
    for ref, value in ((u2_ref, u), (v2_ref, v)):
        high, low = split2(value)
        for j in range(PIECES):
            rows = slice(j * HEADS, (j + 1) * HEADS)
            ref[j] = jnp.concatenate([high[rows], low[rows]], axis=0)
    chosen = lane_heads(HEADS)
    for j in range(PIECES):
        rows = slice(j * HEADS, (j + 1) * HEADS)
        spread = jnp.where(chosen, 0.5 * total[rows], 0.0)
        half_ref[j : j + 1, :] = jnp.sum(spread, axis=0, keepdims=True)

    def piece(j, carry):
        slot = lax.rem(j, slots)
        for copy in reads(j):
            copy.wait()
        u_rows, v_rows = u2_ref[j].T, v2_ref[j].T
        for i in range(TILES):
            us = (cbuf[slot, :, tile(i)].astype(F32) * dot(u_rows, ind_ref[:, tile(i)])).astype(BF16)
            vs = (sbuf[slot, :, tile(i)].astype(F32) * dot(v_rows, ind_ref[:, tile(i)])).astype(BF16)
            us_ref[piece_rows(j), tile(i)] = us
            vs_ref[piece_rows(j), tile(i)] = vs

        @pl.when(j + slots < PIECES)
        def _():
            for copy in reads(j + slots):
                copy.start()

        return carry

    lax.fori_loop(0, PIECES, piece, 0)


def log_rows(*logs):
    lanes = logs[0].shape[1]
    place = iota((16, lanes), 0)
    out = jnp.zeros((16, lanes), F32)
    for i, log in enumerate(logs):
        for k, part in enumerate(split3(log)):
            out = jnp.where(place == 3 * i + k, part.astype(F32), out)
    return out


def log_of(block, i=0):
    return jnp.sum(block[3 * i : 3 * i + 3, :], axis=0, keepdims=True)


def scaled(a):
    most = jnp.maximum(jnp.max(jnp.abs(a), axis=0, keepdims=True), 1e-30)
    return a * (1.0 / most), jnp.log(most)


def state_part(d, us_ref, vs_ref, xt_ref, half_ref, local_ref, after_ref, msg_ref):
    me = lax.rem(lax.axis_index("ctx"), ROW)
    lanes = pl.ds(pl.multiple_of(lax.rem(me + d, ROW) * SLICE, SLICE), SLICE)
    state = jnp.zeros((N, SLICE), F32)
    adjoint = jnp.zeros((N, SLICE), F32)
    total = jnp.zeros((1, SLICE), F32)
    for i in range(PIECES):
        k = PIECES - 1 - i
        local_ref[i, :, lanes] = state.astype(BF16)
        half = half_ref[i : i + 1, lanes]
        weight = jnp.exp(half)
        end = dot(xt_ref[0, :, i * C : (i + 1) * C], vs_ref[i * C : (i + 1) * C, lanes])
        state = weight * (weight * state + end)
        total = total + 2.0 * half
        after_ref[k, :, lanes] = adjoint.astype(BF16)
        weight = jnp.exp(half_ref[k : k + 1, lanes])
        end = dot(xt_ref[1, :, k * C : (k + 1) * C], us_ref[k * C : (k + 1) * C, lanes])
        adjoint = weight * (weight * adjoint + end)
    local_ref[PIECES, :, lanes] = state.astype(BF16)
    msg_ref[0:N, :], first = scaled(state)
    msg_ref[N : 2 * N, :], second = scaled(adjoint)
    msg_ref[2 * N :, :] = log_rows(total, first, second)


def state_kernel(us_ref, vs_ref, r0, r1, r2, r3, other, half_ref, x_ref, xt_ref, local_ref, after_ref, msg_ref):
    z, core, homes = head_places()
    for d, ref in enumerate((r0, r1, r2, r3)):
        x_ref[2 * homes[d] + core] = ref[core]
        x_ref[2 * homes[d] + 1 - core] = other[d]
    for j in range(PIECES):
        rows = slice((j % 2) * C, (j % 2 + 1) * C)
        for i in range(2):
            xt_ref[i, :, j * C : (j + 1) * C] = x_ref[j // 2, i, rows, :].T

    def part(d, carry):
        state_part(d, us_ref, vs_ref, xt_ref, half_ref, local_ref, after_ref, msg_ref.at[d - 1])
        return carry

    lax.fori_loop(1, ROW, part, 0)


def own_state_kernel(us_ref, vs_ref, xt_ref, half_ref, local_in, after_in, local_ref, after_ref, msg_ref):
    state_part(0, us_ref, vs_ref, xt_ref, half_ref, local_ref, after_ref, msg_ref)


def between(logs, places, chosen):
    total = jnp.zeros_like(logs[0])
    for log, place in zip(logs, places):
        total = total + jnp.where(chosen(place), log, 0.0)
    return total


def pick(flag, log):
    return jnp.where(flag, jnp.exp(log), 0.0)


def intra_kernel(us_ref, vs_ref, x_ref, after_ref, base_ref, of_ref):
    of_ref[...] = one_hot(iota((LANES, C), 0) // P_SIZE == iota((LANES, C), 1))
    lower = iota((C, C), 0) >= iota((C, C), 1)

    def piece(j, carry):
        rows = piece_rows(j)
        part = pl.ds(pl.multiple_of(lax.rem(j, 2) * C, C), C)
        block = lax.div(j, 2)
        grad = jnp.where(lower, dot_nt(us_ref[rows, :], vs_ref[rows, :]), 0.0).astype(BF16)
        base_ref[j, 0] = dot_tn(grad, x_ref[block, 1, part, :])
        base_ref[j, 1] = dot(grad, x_ref[block, 0, part, :])
        return carry

    lax.fori_loop(0, PIECES, piece, 0, unroll=2)


def head_places():
    index = lax.axis_index("head")
    z, core = lax.div(index, 2), lax.rem(index, 2)
    return z, core, [lax.rem(z + ROW - d, ROW) for d in range(ROW)]


def own_places():
    index = lax.axis_index("ctx")
    x, y = lax.rem(index, ROW), lax.div(index, ROW)
    return x, y, [lax.rem(x + ROW - d, ROW) for d in range(ROW)]


def row_kernel(r0, r1, r2, r3, base_ref, out_ref):
    x, y, places = own_places()
    refs = (r0, r1, r2, r3)
    ends = [r[2 * N :, :] for r in refs]
    logs = [log_of(end) for end in ends]
    state = jnp.zeros((N, SLICE), F32)
    adjoint = jnp.zeros((N, SLICE), F32)
    for ref, end, own in zip(refs, ends, places):
        state += jnp.exp(between(logs, places, lambda p: p > own) + log_of(end, 1)) * ref[0:N, :]
        adjoint += jnp.exp(between(logs, places, lambda p: p < own) + log_of(end, 2)) * ref[N : 2 * N, :]
    for d in range(1, ROW):
        out_ref[d - 1, 0:N, :], most = scaled(jnp.where(y + d < ROW, state, adjoint))
        out_ref[d - 1, N:, :] = log_rows(sum(logs), most)


def enter_kernel(r0, r1, r2, r3, q1, q2, q3, out_ref):
    x, y, places = own_places()
    refs, rows = (r0, r1, r2, r3), (q1, q2, q3)
    ends = [r[2 * N :, :] for r in refs]
    logs = [log_of(end) for end in ends]
    row_ends = [r[N:, :] for r in rows]
    row_logs = [log_of(end) for end in row_ends]
    row_places = [lax.rem(y + ROW - d, ROW) for d in range(1, ROW)]
    state = jnp.zeros((N, SLICE), F32)
    adjoint = jnp.zeros((N, SLICE), F32)
    for ref, end, own in zip(rows, row_ends, row_places):
        block = ref[0:N, :]
        before = between(row_logs, row_places, lambda p: (p > own) & (p < y)) + log_of(end, 1)
        behind = between(row_logs, row_places, lambda p: (p < own) & (p > y)) + log_of(end, 1)
        state += pick(own < y, before) * block
        adjoint += pick(own > y, behind) * block
    for e in range(ROW):
        to = lax.rem(x + e, ROW)
        first = jnp.exp(between(logs, places, lambda p: p < to)) * state
        second = jnp.exp(between(logs, places, lambda p: p > to)) * adjoint
        for ref, end, own in zip(refs, ends, places):
            before = between(logs, places, lambda p: (p > own) & (p < to)) + log_of(end, 1)
            behind = between(logs, places, lambda p: (p < own) & (p > to)) + log_of(end, 2)
            first += pick(own < to, before) * ref[0:N, :]
            second += pick(own > to, behind) * ref[N : 2 * N, :]
        out_ref[e, 0:N, :], first_log = scaled(first)
        out_ref[e, N : 2 * N, :], second_log = scaled(second)
        out_ref[e, 2 * N :, :] = log_rows(first_log, second_log)


def projection_kernel(
    us_ref,
    vs_ref,
    base_ref,
    half_ref,
    local_ref,
    after_ref,
    s0,
    s1,
    s2,
    s3,
    grad_ref,
    start_ref,
    behind_ref,
    total_ref,
    enter_ref,
    last_ref,
):
    z, core, homes = head_places()
    x, y, places = own_places()
    for ref, place in zip((s0, s1, s2, s3), places):
        lanes = pl.ds(pl.multiple_of(place * SLICE, SLICE), SLICE)
        end = ref[2 * N :, :]
        enter_ref[0, :, lanes] = jnp.exp(log_of(end, 0)) * ref[0:N, :]
        enter_ref[1, :, lanes] = jnp.exp(log_of(end, 1)) * ref[N : 2 * N, :]
    later = jnp.zeros((1, LANES), F32)
    laters = [None] * PIECES
    for j in reversed(range(PIECES)):
        laters[j] = later
        later = later + 2.0 * half_ref[j : j + 1, :]

    prior = jnp.zeros((1, LANES), F32)
    for j in range(PIECES + 1):
        before = jnp.exp(prior)
        if j < PIECES:
            rows = slice(j * C, (j + 1) * C)
            half = half_ref[j : j + 1, :]
            prior = prior + 2.0 * half
            weight, later = jnp.exp(half), jnp.exp(laters[j])
            part = slice((j % 2) * C, (j % 2 + 1) * C)
            to = (lax.rem(j // 4 + ROW - z, ROW), j // 2 % 2)
            grad_out, grad_in = base_ref[j, 1], base_ref[j, 0]
        for i in range(TILES):
            t = tile(i)
            first = local_ref[j, :, t].astype(F32) + before[:, t] * enter_ref[0, :, t]
            if j > 0:
                total_ref[j - 1 : j, t] = jnp.sum(first * last_ref[:, t], axis=0, keepdims=True)
            if j == PIECES:
                continue
            start = (weight[:, t] * first).astype(BF16)
            start_ref[j, :, t] = start
            grad_out = grad_out + dot_nt(us_ref[rows, t], start)
            second = after_ref[j, :, t].astype(F32) + later[:, t] * enter_ref[1, :, t]
            last_ref[:, t] = second
            behind = (weight[:, t] * second).astype(BF16)
            behind_ref[j, :, t] = behind
            grad_in = grad_in + dot_nt(vs_ref[rows, t], behind)
        if j < PIECES:
            grad_ref[*to, 1, part, :] = grad_out.astype(BF16)
            grad_ref[*to, 0, part, :] = grad_in.astype(BF16)


def result_kernel(
    us_ref,
    vs_ref,
    start_ref,
    behind_ref,
    x_ref,
    u2_ref,
    v2_ref,
    out_hbm,
    grad_hbm,
    diff_ref,
    obuf,
    gbuf,
    ind_ref,
    osem,
    gsem,
):
    outs = obuf.shape[0]

    def writes(j):
        slot = lax.rem(j, outs)
        return (
            pltpu.make_async_copy(obuf.at[slot], out_hbm.at[piece_rows(j)], osem.at[slot]),
            pltpu.make_async_copy(gbuf.at[slot], grad_hbm.at[piece_rows(j)], gsem.at[slot]),
        )

    ind_ref[...] = one_hot(lane_heads(2 * HEADS))
    lower = iota((C, C), 0) >= iota((C, C), 1)
    upper = iota((C, C), 0) <= iota((C, C), 1)

    def piece(j, carry):
        place = lax.rem(j, outs)
        part = pl.ds(pl.multiple_of(lax.rem(j, 2) * C, C), C)
        block = lax.div(j, 2)
        x_in, x_out = x_ref[block, 0, part, :], x_ref[block, 1, part, :]
        scores = jnp.where(lower, dot_nt(x_out, x_in), 0.0).astype(BF16)
        turned = jnp.where(upper, dot_nt(x_in, x_out), 0.0).astype(BF16)
        u_rows, v_rows = u2_ref[j].T, v2_ref[j].T
        left_out = jnp.concatenate([scores, x_out], axis=1)
        left_grad = jnp.concatenate([turned, x_in], axis=1)

        @pl.when(j >= outs)
        def _():
            for copy in writes(j - outs):
                copy.wait()

        for i in range(TILES):
            us, vs = us_ref[piece_rows(j), tile(i)], vs_ref[piece_rows(j), tile(i)]
            out = dot(left_out, jnp.concatenate([vs, start_ref[j, :, tile(i)]], axis=0))
            obuf[place, :, tile(i)] = (out * dot(u_rows, ind_ref[:, tile(i)])).astype(BF16)
            grad = dot(left_grad, jnp.concatenate([us, behind_ref[j, :, tile(i)]], axis=0))
            gbuf[place, :, tile(i)] = (grad * dot(v_rows, ind_ref[:, tile(i)])).astype(BF16)
            diff = us.astype(F32) * out - vs.astype(F32) * grad
            diff_ref[piece_rows(j), tile(i)] = diff.astype(BF16)
        for copy in writes(j):
            copy.start()
        return carry

    lax.fori_loop(0, PIECES, piece, 0, unroll=2)
    for j in range(PIECES - outs, PIECES):
        for copy in writes(j):
            copy.wait()


def decay_part(k, diff_ref, heads_ref, of_ref, decay_ref):
    from_on = one_hot(iota((C, C), 0) >= iota((C, C), 1))
    last = iota((HEADS, C), 1) == C - 1
    cum_grad = dot(diff_ref[4 * k * C : 4 * (k + 1) * C, :], of_ref[...])
    parts = []
    for j in range(4):
        total = heads_ref[:, 4 * k + j : 4 * k + j + 1]
        parts.append(cum_grad[j * C : (j + 1) * C].T[0:HEADS] + jnp.where(last, total, 0.0))
    sums = sum(dot(part, from_on) for part in split3(jnp.concatenate(parts, axis=0)))
    for j in range(4):
        decay_ref[:, (4 * k + j) * C : (4 * k + j + 1) * C] = sums[j * HEADS : (j + 1) * HEADS]


def first_decay_kernel(diff_ref, total_ref, of_ref, decay_ref, heads_ref):
    own = one_hot(lane_heads(HEADS))
    heads_ref[...] = sum(dot_nt(own, part) for part in split3(total_ref[...]))
    for k in range(2):
        decay_part(k, diff_ref, heads_ref, of_ref, decay_ref)


def decay_kernel(diff_ref, heads_ref, of_ref, first_ref, decay_ref):
    decay_ref[:, 0 : TOKENS // 2] = first_ref[...]
    for k in range(2, 4):
        decay_part(k, diff_ref, heads_ref, of_ref, decay_ref)


def split_copies(d, in_hbm, out_hbm, ref, sems):
    z, core, homes = head_places()
    copies = []
    for to in range(2):
        group = 2 * lax.rem(z + d, ROW) + to
        columns = pl.ds(pl.multiple_of(group * N, N), N)
        for i, source in enumerate((in_hbm, out_hbm)):
            copies.append(pltpu.make_async_copy(source.at[:, columns], ref.at[to, i], sems.at[d, to, i]))
    return copies


def far_kernel(in_hbm, out_hbm, ld_hbm, s2, ld_ref, sems, sem):
    copies = split_copies(2, in_hbm, out_hbm, s2, sems) + [pltpu.make_async_copy(ld_hbm, ld_ref, sem)]
    for copy in copies:
        copy.start()
    for copy in copies:
        copy.wait()


def split_kernel(in_hbm, out_hbm, s2, s0, s1, s3, sems):
    copies = []
    for d, ref in ((1, s1), (3, s3), (0, s0)):
        copies += split_copies(d, in_hbm, out_hbm, ref, sems)
    for copy in copies:
        copy.start()
    for copy in copies:
        copy.wait()


def swap_kernel(r0, r1, r2, r3, after_hbm, other_ref):
    z, core, homes = head_places()
    for d, ref in enumerate((r0, r1, r2, r3)):
        other_ref[d] = ref[1 - core]


def join_kernel(r0, r1, r2, r3, other, after_hbm, in_hbm, out_hbm, sems):
    z, core, homes = head_places()
    copies = []
    for d, ref in enumerate((r0, r1, r2, r3)):
        for k, (source, of_core) in enumerate(((ref.at[core], core), (other.at[d], 1 - core))):
            columns = pl.ds(pl.multiple_of((2 * homes[d] + of_core) * N, N), N)
            for i, result in enumerate((in_hbm, out_hbm)):
                copies.append(pltpu.make_async_copy(source.at[i], result.at[:, columns], sems.at[d, k, i]))
    for copy in copies:
        copy.start()
    for copy in copies:
        copy.wait()


VMEM = pl.BlockSpec(memory_space=pltpu.VMEM)
HBM = pl.BlockSpec(memory_space=pltpu.HBM)
DMA = pltpu.SemaphoreType.DMA


def call(kernel, args, outs, specs, out_specs, scratch=(), limit=10, flops=0, moved=0, aliases={}):
    return pl.pallas_call(
        kernel,
        out_shape=outs,
        in_specs=specs,
        out_specs=out_specs,
        scratch_shapes=list(scratch),
        input_output_aliases=aliases,
        compiler_params=pltpu.CompilerParams(vmem_limit_bytes=limit * MIB),
        cost_estimate=pl.CostEstimate(flops=flops, bytes_accessed=moved, transcendentals=0),
    )(*args)


def held(shape, dtype=BF16):
    return pltpu.VMEM(shape, dtype)


def far(a):
    return pltpu.with_memory_space_constraint(a, pltpu.HBM)


def kept(shape, dtype=BF16):
    return pltpu.HBM(shape, dtype)


def plain(shape, dtype=BF16):
    return jax.ShapeDtypeStruct(shape, dtype)


def along_x(d):
    return [(y * ROW + x, y * ROW + (x + d) % ROW) for y in range(ROW) for x in range(ROW)]


def along_y(d):
    return [(y * ROW + x, (y + d) % ROW * ROW + x) for y in range(ROW) for x in range(ROW)]


def along_z(d):
    return [(z * 2 + c, (z + d) % ROW * 2 + c) for z in range(ROW) for c in range(2)]


def send(a, pairs):
    return lax.ppermute(a.astype(jnp.float16), "ctx", pairs).astype(F32)


OTHER_CORE = [(i, i ^ 1) for i in range(2 * ROW)]


def body(signal, log_decay, state_in, state_out, cotangent):
    own = state_in.shape[0]
    chip = (2, 2, own, N)
    blocks = (2 * ROW, 2, own, N)
    wide = (TOKENS, LANES)
    states = (PIECES, N, LANES)
    band = (C, LANES)

    marks = DMA((ROW, 2, 2))
    s2, decays = call(
        far_kernel,
        (far(state_in), far(state_out), far(log_decay)),
        (held(chip), held(log_decay.shape, F32)),
        [HBM] * 3,
        [VMEM] * 2,
        [marks, DMA],
    )
    r2 = lax.ppermute(s2, "head", along_z(2))
    s0, s1, s3 = call(
        split_kernel, (far(state_in), far(state_out), s2), [held(chip)] * 3, [HBM] * 2 + [VMEM], [VMEM] * 3, [marks]
    )
    got = [s0, lax.ppermute(s1, "head", along_z(1)), r2, lax.ppermute(s3, "head", along_z(3))]
    us, vs, u2, v2, half = call(
        scale_kernel,
        (far(signal), far(cotangent), decays),
        (
            held(wide),
            held(wide),
            held((PIECES, 2 * HEADS, C)),
            held((PIECES, 2 * HEADS, C)),
            held((PIECES, LANES), F32),
        ),
        [HBM, HBM, VMEM],
        [VMEM] * 5,
        [pltpu.VMEM((2 * HEADS, LANES), BF16)] + [pltpu.VMEM((4,) + band, BF16)] * 2 + [DMA((4,))] * 2,
        flops=1 << 33,
        moved=1 << 23,
    )
    other = call(swap_kernel, got + [half], held((ROW, 2, own, N)), [VMEM] * 5, VMEM)
    other = lax.ppermute(other, "head", OTHER_CORE)
    x, xt, local, after, msg = call(
        state_kernel,
        [us, vs] + got + [other, half],
        (
            held(blocks),
            held((2, N, TOKENS)),
            held((PIECES + 1, N, LANES)),
            held(states),
            held((ROW - 1, 2 * N + 16, SLICE), F32),
        ),
        [VMEM] * 8,
        [VMEM] * 5,
    )
    mates = [send(msg[d - 1], along_x(d)) for d in range(1, ROW)]
    local, after, own_msg = call(
        own_state_kernel,
        (us, vs, xt, half, local, after),
        (held((PIECES + 1, N, LANES)), held(states), held((2 * N + 16, SLICE), F32)),
        [VMEM] * 6,
        [VMEM] * 3,
        aliases={4: 0, 5: 1},
        flops=1 << 31,
        moved=1 << 23,
    )
    mates = [own_msg] + mates
    base, of_head = call(
        intra_kernel,
        (us, vs, x, local),
        (held((PIECES, 2, C, N), F32), held((LANES, C))),
        [VMEM] * 4,
        [VMEM] * 2,
        flops=1 << 33,
        moved=1 << 23,
    )
    row_totals = call(row_kernel, mates + [base], held((ROW - 1, N + 16, SLICE), F32), [VMEM] * 5, VMEM)
    rows = [send(row_totals[d - 1], along_y(d)) for d in range(1, ROW)]
    back = call(enter_kernel, mates + rows, held((ROW, 2 * N + 16, SLICE), F32), [VMEM] * 7, VMEM)
    shares = [back[0]] + [send(back[e], along_x(e)) for e in range(1, ROW)]
    grads, start, behind, total = call(
        projection_kernel,
        [us, vs, base, half, local, after] + shares,
        (held((ROW,) + chip), held(states), held(states), held((PIECES, LANES), F32)),
        [VMEM] * 10,
        [VMEM] * 4,
        [pltpu.VMEM((2,) + band, F32), pltpu.VMEM(band, F32)],
    )
    returned = [grads[0]] + [lax.ppermute(grads[d], "head", along_z(d)) for d in (1, 3, 2)]
    returned = [returned[0], returned[1], returned[3], returned[2]]
    output, grad_signal, diff = call(
        result_kernel,
        (us, vs, start, behind, x, u2, v2),
        (plain(wide), plain(wide), held(wide)),
        [VMEM] * 7,
        [HBM, HBM, VMEM],
        [pltpu.VMEM((4,) + band, BF16)] * 2 + [pltpu.VMEM((2 * HEADS, LANES), BF16), DMA((4,)), DMA((4,))],
        flops=1 << 34,
        moved=1 << 23,
    )
    decay, totals = call(
        first_decay_kernel,
        (diff, total, of_head),
        (held((HEADS, TOKENS // 2), F32), held((HEADS, PIECES), F32)),
        [VMEM] * 3,
        [VMEM] * 2,
    )
    other = call(swap_kernel, returned + [decay], held((ROW, 2, own, N)), [VMEM] * 5, VMEM)
    other = lax.ppermute(other, "head", OTHER_CORE)
    grad_decay = call(
        decay_kernel, (diff, totals, of_head, decay), plain((HEADS, TOKENS), F32), [VMEM] * 4, VMEM, flops=1 << 31, moved=1 << 22
    )
    narrow = plain(state_in.shape)
    grad_in, grad_out = call(
        join_kernel, returned + [other, far(grad_decay)], (narrow, narrow), [VMEM] * 5 + [HBM], [HBM] * 2, [marks]
    )
    return output, grad_signal, grad_in, grad_out, grad_decay


def solution(mesh):
    in_specs = (
        P("ctx", "head"),
        P("head", "ctx"),
        P(("ctx", "head"), None),
        P(("ctx", "head"), None),
        P("ctx", "head"),
    )
    out_specs = (
        P("ctx", "head"),
        P("ctx", "head"),
        P(("ctx", "head"), None),
        P(("ctx", "head"), None),
        P("head", "ctx"),
    )
    return jax.shard_map(body, mesh=mesh, in_specs=in_specs, out_specs=out_specs, check_vma=False)
```

```python
import jax
import jax.numpy as jnp
from jax import lax
from jax.experimental import pallas as pl
from jax.experimental.pallas import tpu as pltpu
from jax.sharding import PartitionSpec as P

HEADS = 16
P_SIZE = 64
N = 128
C = 128
LANES = HEADS * P_SIZE
TOKENS = 2048
PIECES = TOKENS // C
ROW = 4
SLICE = LANES // ROW
MIB = 1 << 20

F32 = jnp.float32
BF16 = jnp.bfloat16


def dot(a, b):
    return lax.dot_general(a, b, (((1,), (0,)), ((), ())), preferred_element_type=F32)


def dot_nt(a, b):
    return lax.dot_general(a, b, (((1,), (1,)), ((), ())), preferred_element_type=F32)


def dot_tn(a, b):
    return lax.dot_general(a, b, (((0,), (0,)), ((), ())), preferred_element_type=F32)


def split2(a):
    high = a.astype(BF16)
    return high, (a - high.astype(F32)).astype(BF16)


def split3(a):
    high = a.astype(BF16)
    rest = a - high.astype(F32)
    return (high,) + split2(rest)


def iota(shape, dim):
    return lax.broadcasted_iota(jnp.int32, shape, dim)


def lane_heads(rows):
    return (iota((rows, LANES), 1) // P_SIZE) == (iota((rows, LANES), 0) % HEADS)


def one_hot(chosen):
    return jnp.where(chosen, 1.0, 0.0).astype(BF16)


TILES = 4
TILE = LANES // TILES


def tile(i):
    return slice(i * TILE, (i + 1) * TILE)


def piece_rows(j):
    return pl.ds(pl.multiple_of(j * C, C), C)


def scale_kernel(
    sig_hbm, cot_hbm, ld_ref, us_ref, vs_ref, u2_ref, v2_ref, half_ref, ind_ref, sbuf, cbuf, ssem, csem
):
    slots = sbuf.shape[0]

    def reads(j):
        slot = lax.rem(j, slots)
        return (
            pltpu.make_async_copy(sig_hbm.at[piece_rows(j)], sbuf.at[slot], ssem.at[slot]),
            pltpu.make_async_copy(cot_hbm.at[piece_rows(j)], cbuf.at[slot], csem.at[slot]),
        )

    for j in range(slots):
        for copy in reads(j):
            copy.start()

    ind_ref[...] = one_hot(lane_heads(2 * HEADS))
    decay = jnp.concatenate([ld_ref[:, j * C : (j + 1) * C] for j in range(PIECES)], axis=0)
    upto = one_hot(iota((C, C), 0) <= iota((C, C), 1))
    cum = sum(dot(part, upto) for part in split3(decay))
    total = cum[:, C - 1 : C]
    u = jnp.exp(cum - 0.5 * total)
    v = jnp.exp(0.5 * total - cum)
    for ref, value in ((u2_ref, u), (v2_ref, v)):
        high, low = split2(value)
        for j in range(PIECES):
            rows = slice(j * HEADS, (j + 1) * HEADS)
            ref[j] = jnp.concatenate([high[rows], low[rows]], axis=0)
    chosen = lane_heads(HEADS)
    for j in range(PIECES):
        rows = slice(j * HEADS, (j + 1) * HEADS)
        spread = jnp.where(chosen, 0.5 * total[rows], 0.0)
        half_ref[j : j + 1, :] = jnp.sum(spread, axis=0, keepdims=True)

    def piece(j, carry):
        slot = lax.rem(j, slots)
        for copy in reads(j):
            copy.wait()
        u_rows, v_rows = u2_ref[j].T, v2_ref[j].T
        for i in range(TILES):
            us = (cbuf[slot, :, tile(i)].astype(F32) * dot(u_rows, ind_ref[:, tile(i)])).astype(BF16)
            vs = (sbuf[slot, :, tile(i)].astype(F32) * dot(v_rows, ind_ref[:, tile(i)])).astype(BF16)
            us_ref[piece_rows(j), tile(i)] = us
            vs_ref[piece_rows(j), tile(i)] = vs

        @pl.when(j + slots < PIECES)
        def _():
            for copy in reads(j + slots):
                copy.start()

        return carry

    lax.fori_loop(0, PIECES, piece, 0)


def log_rows(*logs):
    lanes = logs[0].shape[1]
    place = iota((16, lanes), 0)
    out = jnp.zeros((16, lanes), F32)
    for i, log in enumerate(logs):
        for k, part in enumerate(split3(log)):
            out = jnp.where(place == 3 * i + k, part.astype(F32), out)
    return out


def log_of(block, i=0):
    return jnp.sum(block[3 * i : 3 * i + 3, :], axis=0, keepdims=True)


def scaled(a):
    most = jnp.maximum(jnp.max(jnp.abs(a), axis=0, keepdims=True), 1e-30)
    return a * (1.0 / most), jnp.log(most)


def state_part(d, us_ref, vs_ref, xt_ref, half_ref, local_ref, after_ref, msg_ref):
    me = lax.rem(lax.axis_index("ctx"), ROW)
    lanes = pl.ds(pl.multiple_of(lax.rem(me + d, ROW) * SLICE, SLICE), SLICE)
    state = jnp.zeros((N, SLICE), F32)
    adjoint = jnp.zeros((N, SLICE), F32)
    total = jnp.zeros((1, SLICE), F32)
    for i in range(PIECES):
        k = PIECES - 1 - i
        local_ref[i, :, lanes] = state.astype(BF16)
        half = half_ref[i : i + 1, lanes]
        weight = jnp.exp(half)
        end = dot(xt_ref[0, :, i * C : (i + 1) * C], vs_ref[i * C : (i + 1) * C, lanes])
        state = weight * (weight * state + end)
        total = total + 2.0 * half
        after_ref[k, :, lanes] = adjoint.astype(BF16)
        weight = jnp.exp(half_ref[k : k + 1, lanes])
        end = dot(xt_ref[1, :, k * C : (k + 1) * C], us_ref[k * C : (k + 1) * C, lanes])
        adjoint = weight * (weight * adjoint + end)
    local_ref[PIECES, :, lanes] = state.astype(BF16)
    msg_ref[0:N, :], first = scaled(state)
    msg_ref[N : 2 * N, :], second = scaled(adjoint)
    msg_ref[2 * N :, :] = log_rows(total, first, second)


def state_kernel(us_ref, vs_ref, r0, r1, r2, r3, other, half_ref, x_ref, xt_ref, local_ref, after_ref, msg_ref):
    z, core, homes = head_places()
    for d, ref in enumerate((r0, r1, r2, r3)):
        x_ref[2 * homes[d] + core] = ref[core]
        x_ref[2 * homes[d] + 1 - core] = other[d]
    for j in range(PIECES):
        rows = slice((j % 2) * C, (j % 2 + 1) * C)
        for i in range(2):
            xt_ref[i, :, j * C : (j + 1) * C] = x_ref[j // 2, i, rows, :].T

    def part(d, carry):
        state_part(d, us_ref, vs_ref, xt_ref, half_ref, local_ref, after_ref, msg_ref.at[d - 1])
        return carry

    lax.fori_loop(1, ROW, part, 0)


def own_state_kernel(us_ref, vs_ref, xt_ref, half_ref, local_in, after_in, local_ref, after_ref, msg_ref):
    state_part(0, us_ref, vs_ref, xt_ref, half_ref, local_ref, after_ref, msg_ref)


def between(logs, places, chosen):
    total = jnp.zeros_like(logs[0])
    for log, place in zip(logs, places):
        total = total + jnp.where(chosen(place), log, 0.0)
    return total


def pick(flag, log):
    return jnp.where(flag, jnp.exp(log), 0.0)


def intra_kernel(us_ref, vs_ref, x_ref, after_ref, base_ref, of_ref):
    of_ref[...] = one_hot(iota((LANES, C), 0) // P_SIZE == iota((LANES, C), 1))
    lower = iota((C, C), 0) >= iota((C, C), 1)

    def piece(j, carry):
        rows = piece_rows(j)
        part = pl.ds(pl.multiple_of(lax.rem(j, 2) * C, C), C)
        block = lax.div(j, 2)
        grad = jnp.where(lower, dot_nt(us_ref[rows, :], vs_ref[rows, :]), 0.0).astype(BF16)
        base_ref[j, 0] = dot_tn(grad, x_ref[block, 1, part, :])
        base_ref[j, 1] = dot(grad, x_ref[block, 0, part, :])
        return carry

    lax.fori_loop(0, PIECES, piece, 0, unroll=2)


def head_places():
    index = lax.axis_index("head")
    z, core = lax.div(index, 2), lax.rem(index, 2)
    return z, core, [lax.rem(z + ROW - d, ROW) for d in range(ROW)]


def own_places():
    index = lax.axis_index("ctx")
    x, y = lax.rem(index, ROW), lax.div(index, ROW)
    return x, y, [lax.rem(x + ROW - d, ROW) for d in range(ROW)]


def row_kernel(r0, r1, r2, r3, base_ref, out_ref):
    x, y, places = own_places()
    refs = (r0, r1, r2, r3)
    ends = [r[2 * N :, :] for r in refs]
    logs = [log_of(end) for end in ends]
    state = jnp.zeros((N, SLICE), F32)
    adjoint = jnp.zeros((N, SLICE), F32)
    for ref, end, own in zip(refs, ends, places):
        state += jnp.exp(between(logs, places, lambda p: p > own) + log_of(end, 1)) * ref[0:N, :]
        adjoint += jnp.exp(between(logs, places, lambda p: p < own) + log_of(end, 2)) * ref[N : 2 * N, :]
    for d in range(1, ROW):
        out_ref[d - 1, 0:N, :], most = scaled(jnp.where(y + d < ROW, state, adjoint))
        out_ref[d - 1, N:, :] = log_rows(sum(logs), most)


def enter_kernel(r0, r1, r2, r3, q1, q2, q3, out_ref):
    x, y, places = own_places()
    refs, rows = (r0, r1, r2, r3), (q1, q2, q3)
    ends = [r[2 * N :, :] for r in refs]
    logs = [log_of(end) for end in ends]
    row_ends = [r[N:, :] for r in rows]
    row_logs = [log_of(end) for end in row_ends]
    row_places = [lax.rem(y + ROW - d, ROW) for d in range(1, ROW)]
    state = jnp.zeros((N, SLICE), F32)
    adjoint = jnp.zeros((N, SLICE), F32)
    for ref, end, own in zip(rows, row_ends, row_places):
        block = ref[0:N, :]
        before = between(row_logs, row_places, lambda p: (p > own) & (p < y)) + log_of(end, 1)
        behind = between(row_logs, row_places, lambda p: (p < own) & (p > y)) + log_of(end, 1)
        state += pick(own < y, before) * block
        adjoint += pick(own > y, behind) * block
    for e in range(ROW):
        to = lax.rem(x + e, ROW)
        first = jnp.exp(between(logs, places, lambda p: p < to)) * state
        second = jnp.exp(between(logs, places, lambda p: p > to)) * adjoint
        for ref, end, own in zip(refs, ends, places):
            before = between(logs, places, lambda p: (p > own) & (p < to)) + log_of(end, 1)
            behind = between(logs, places, lambda p: (p < own) & (p > to)) + log_of(end, 2)
            first += pick(own < to, before) * ref[0:N, :]
            second += pick(own > to, behind) * ref[N : 2 * N, :]
        out_ref[e, 0:N, :], first_log = scaled(first)
        out_ref[e, N : 2 * N, :], second_log = scaled(second)
        out_ref[e, 2 * N :, :] = log_rows(first_log, second_log)


def projection_kernel(
    us_ref,
    vs_ref,
    base_ref,
    half_ref,
    local_ref,
    after_ref,
    s0,
    s1,
    s2,
    s3,
    grad_ref,
    start_ref,
    behind_ref,
    total_ref,
    enter_ref,
    last_ref,
):
    z, core, homes = head_places()
    x, y, places = own_places()
    for ref, place in zip((s0, s1, s2, s3), places):
        lanes = pl.ds(pl.multiple_of(place * SLICE, SLICE), SLICE)
        end = ref[2 * N :, :]
        enter_ref[0, :, lanes] = jnp.exp(log_of(end, 0)) * ref[0:N, :]
        enter_ref[1, :, lanes] = jnp.exp(log_of(end, 1)) * ref[N : 2 * N, :]
    later = jnp.zeros((1, LANES), F32)
    laters = [None] * PIECES
    for j in reversed(range(PIECES)):
        laters[j] = later
        later = later + 2.0 * half_ref[j : j + 1, :]

    prior = jnp.zeros((1, LANES), F32)
    for j in range(PIECES + 1):
        before = jnp.exp(prior)
        if j < PIECES:
            rows = slice(j * C, (j + 1) * C)
            half = half_ref[j : j + 1, :]
            prior = prior + 2.0 * half
            weight, later = jnp.exp(half), jnp.exp(laters[j])
            part = slice((j % 2) * C, (j % 2 + 1) * C)
            to = (lax.rem(j // 4 + ROW - z, ROW), j // 2 % 2)
            grad_out, grad_in = base_ref[j, 1], base_ref[j, 0]
        for i in range(TILES):
            t = tile(i)
            first = local_ref[j, :, t].astype(F32) + before[:, t] * enter_ref[0, :, t]
            if j > 0:
                total_ref[j - 1 : j, t] = jnp.sum(first * last_ref[:, t], axis=0, keepdims=True)
            if j == PIECES:
                continue
            start = (weight[:, t] * first).astype(BF16)
            start_ref[j, :, t] = start
            grad_out = grad_out + dot_nt(us_ref[rows, t], start)
            second = after_ref[j, :, t].astype(F32) + later[:, t] * enter_ref[1, :, t]
            last_ref[:, t] = second
            behind = (weight[:, t] * second).astype(BF16)
            behind_ref[j, :, t] = behind
            grad_in = grad_in + dot_nt(vs_ref[rows, t], behind)
        if j < PIECES:
            grad_ref[*to, 1, part, :] = grad_out.astype(BF16)
            grad_ref[*to, 0, part, :] = grad_in.astype(BF16)


def result_kernel(
    us_ref,
    vs_ref,
    start_ref,
    behind_ref,
    x_ref,
    u2_ref,
    v2_ref,
    out_hbm,
    grad_hbm,
    diff_ref,
    obuf,
    gbuf,
    ind_ref,
    osem,
    gsem,
):
    outs = obuf.shape[0]

    def writes(j):
        slot = lax.rem(j, outs)
        return (
            pltpu.make_async_copy(obuf.at[slot], out_hbm.at[piece_rows(j)], osem.at[slot]),
            pltpu.make_async_copy(gbuf.at[slot], grad_hbm.at[piece_rows(j)], gsem.at[slot]),
        )

    ind_ref[...] = one_hot(lane_heads(2 * HEADS))
    lower = iota((C, C), 0) >= iota((C, C), 1)
    upper = iota((C, C), 0) <= iota((C, C), 1)

    def piece(j, carry):
        place = lax.rem(j, outs)
        part = pl.ds(pl.multiple_of(lax.rem(j, 2) * C, C), C)
        block = lax.div(j, 2)
        x_in, x_out = x_ref[block, 0, part, :], x_ref[block, 1, part, :]
        scores = jnp.where(lower, dot_nt(x_out, x_in), 0.0).astype(BF16)
        turned = jnp.where(upper, dot_nt(x_in, x_out), 0.0).astype(BF16)
        u_rows, v_rows = u2_ref[j].T, v2_ref[j].T
        left_out = jnp.concatenate([scores, x_out], axis=1)
        left_grad = jnp.concatenate([turned, x_in], axis=1)

        @pl.when(j >= outs)
        def _():
            for copy in writes(j - outs):
                copy.wait()

        for i in range(TILES):
            us, vs = us_ref[piece_rows(j), tile(i)], vs_ref[piece_rows(j), tile(i)]
            out = dot(left_out, jnp.concatenate([vs, start_ref[j, :, tile(i)]], axis=0))
            obuf[place, :, tile(i)] = (out * dot(u_rows, ind_ref[:, tile(i)])).astype(BF16)
            grad = dot(left_grad, jnp.concatenate([us, behind_ref[j, :, tile(i)]], axis=0))
            gbuf[place, :, tile(i)] = (grad * dot(v_rows, ind_ref[:, tile(i)])).astype(BF16)
            diff = us.astype(F32) * out - vs.astype(F32) * grad
            diff_ref[piece_rows(j), tile(i)] = diff.astype(BF16)
        for copy in writes(j):
            copy.start()
        return carry

    lax.fori_loop(0, PIECES, piece, 0, unroll=4)
    for j in range(PIECES - outs, PIECES):
        for copy in writes(j):
            copy.wait()


def decay_part(k, diff_ref, heads_ref, of_ref, decay_ref):
    from_on = one_hot(iota((C, C), 0) >= iota((C, C), 1))
    last = iota((HEADS, C), 1) == C - 1
    cum_grad = dot(diff_ref[4 * k * C : 4 * (k + 1) * C, :], of_ref[...])
    parts = []
    for j in range(4):
        total = heads_ref[:, 4 * k + j : 4 * k + j + 1]
        parts.append(cum_grad[j * C : (j + 1) * C].T[0:HEADS] + jnp.where(last, total, 0.0))
    sums = sum(dot(part, from_on) for part in split3(jnp.concatenate(parts, axis=0)))
    for j in range(4):
        decay_ref[:, (4 * k + j) * C : (4 * k + j + 1) * C] = sums[j * HEADS : (j + 1) * HEADS]


def first_decay_kernel(diff_ref, total_ref, of_ref, decay_ref, heads_ref):
    own = one_hot(lane_heads(HEADS))
    heads_ref[...] = sum(dot_nt(own, part) for part in split3(total_ref[...]))
    for k in range(2):
        decay_part(k, diff_ref, heads_ref, of_ref, decay_ref)


def decay_kernel(diff_ref, heads_ref, of_ref, first_ref, decay_ref):
    decay_ref[:, 0 : TOKENS // 2] = first_ref[...]
    for k in range(2, 4):
        decay_part(k, diff_ref, heads_ref, of_ref, decay_ref)


def split_copies(d, in_hbm, out_hbm, ref, sems):
    z, core, homes = head_places()
    copies = []
    for to in range(2):
        group = 2 * lax.rem(z + d, ROW) + to
        columns = pl.ds(pl.multiple_of(group * N, N), N)
        for i, source in enumerate((in_hbm, out_hbm)):
            copies.append(pltpu.make_async_copy(source.at[:, columns], ref.at[to, i], sems.at[d, to, i]))
    return copies


def far_kernel(in_hbm, out_hbm, ld_hbm, s2, ld_ref, sems, sem):
    copies = split_copies(2, in_hbm, out_hbm, s2, sems) + [pltpu.make_async_copy(ld_hbm, ld_ref, sem)]
    for copy in copies:
        copy.start()
    for copy in copies:
        copy.wait()


def split_kernel(in_hbm, out_hbm, s2, s0, s1, s3, sems):
    copies = []
    for d, ref in ((1, s1), (3, s3), (0, s0)):
        copies += split_copies(d, in_hbm, out_hbm, ref, sems)
    for copy in copies:
        copy.start()
    for copy in copies:
        copy.wait()


def swap_kernel(r0, r1, r2, r3, after_hbm, other_ref):
    z, core, homes = head_places()
    for d, ref in enumerate((r0, r1, r2, r3)):
        other_ref[d] = ref[1 - core]


def join_kernel(r0, r1, r2, r3, other, after_hbm, in_hbm, out_hbm, sems):
    z, core, homes = head_places()
    copies = []
    for d, ref in enumerate((r0, r1, r2, r3)):
        for k, (source, of_core) in enumerate(((ref.at[core], core), (other.at[d], 1 - core))):
            columns = pl.ds(pl.multiple_of((2 * homes[d] + of_core) * N, N), N)
            for i, result in enumerate((in_hbm, out_hbm)):
                copies.append(pltpu.make_async_copy(source.at[i], result.at[:, columns], sems.at[d, k, i]))
    for copy in copies:
        copy.start()
    for copy in copies:
        copy.wait()


VMEM = pl.BlockSpec(memory_space=pltpu.VMEM)
HBM = pl.BlockSpec(memory_space=pltpu.HBM)
DMA = pltpu.SemaphoreType.DMA


def call(kernel, args, outs, specs, out_specs, scratch=(), limit=10, flops=0, moved=0, aliases={}):
    return pl.pallas_call(
        kernel,
        out_shape=outs,
        in_specs=specs,
        out_specs=out_specs,
        scratch_shapes=list(scratch),
        input_output_aliases=aliases,
        compiler_params=pltpu.CompilerParams(vmem_limit_bytes=limit * MIB),
        cost_estimate=pl.CostEstimate(flops=flops, bytes_accessed=moved, transcendentals=0),
    )(*args)


def held(shape, dtype=BF16):
    return pltpu.VMEM(shape, dtype)


def far(a):
    return pltpu.with_memory_space_constraint(a, pltpu.HBM)


def kept(shape, dtype=BF16):
    return pltpu.HBM(shape, dtype)


def plain(shape, dtype=BF16):
    return jax.ShapeDtypeStruct(shape, dtype)


def along_x(d):
    return [(y * ROW + x, y * ROW + (x + d) % ROW) for y in range(ROW) for x in range(ROW)]


def along_y(d):
    return [(y * ROW + x, (y + d) % ROW * ROW + x) for y in range(ROW) for x in range(ROW)]


def along_z(d):
    return [(z * 2 + c, (z + d) % ROW * 2 + c) for z in range(ROW) for c in range(2)]


def send(a, pairs):
    return lax.ppermute(a.astype(jnp.float16), "ctx", pairs).astype(F32)


OTHER_CORE = [(i, i ^ 1) for i in range(2 * ROW)]


def body(signal, log_decay, state_in, state_out, cotangent):
    own = state_in.shape[0]
    chip = (2, 2, own, N)
    blocks = (2 * ROW, 2, own, N)
    wide = (TOKENS, LANES)
    states = (PIECES, N, LANES)
    band = (C, LANES)

    marks = DMA((ROW, 2, 2))
    s2, decays = call(
        far_kernel,
        (far(state_in), far(state_out), far(log_decay)),
        (held(chip), held(log_decay.shape, F32)),
        [HBM] * 3,
        [VMEM] * 2,
        [marks, DMA],
    )
    r2 = lax.ppermute(s2, "head", along_z(2))
    s0, s1, s3 = call(
        split_kernel, (far(state_in), far(state_out), s2), [held(chip)] * 3, [HBM] * 2 + [VMEM], [VMEM] * 3, [marks]
    )
    got = [s0, lax.ppermute(s1, "head", along_z(1)), r2, lax.ppermute(s3, "head", along_z(3))]
    us, vs, u2, v2, half = call(
        scale_kernel,
        (far(signal), far(cotangent), decays),
        (
            held(wide),
            held(wide),
            held((PIECES, 2 * HEADS, C)),
            held((PIECES, 2 * HEADS, C)),
            held((PIECES, LANES), F32),
        ),
        [HBM, HBM, VMEM],
        [VMEM] * 5,
        [pltpu.VMEM((2 * HEADS, LANES), BF16)] + [pltpu.VMEM((4,) + band, BF16)] * 2 + [DMA((4,))] * 2,
        flops=1 << 33,
        moved=1 << 23,
    )
    other = call(swap_kernel, got + [half], held((ROW, 2, own, N)), [VMEM] * 5, VMEM)
    other = lax.ppermute(other, "head", OTHER_CORE)
    x, xt, local, after, msg = call(
        state_kernel,
        [us, vs] + got + [other, half],
        (
            held(blocks),
            held((2, N, TOKENS)),
            held((PIECES + 1, N, LANES)),
            held(states),
            held((ROW - 1, 2 * N + 16, SLICE), F32),
        ),
        [VMEM] * 8,
        [VMEM] * 5,
    )
    mates = [send(msg[d - 1], along_x(d)) for d in range(1, ROW)]
    local, after, own_msg = call(
        own_state_kernel,
        (us, vs, xt, half, local, after),
        (held((PIECES + 1, N, LANES)), held(states), held((2 * N + 16, SLICE), F32)),
        [VMEM] * 6,
        [VMEM] * 3,
        aliases={4: 0, 5: 1},
        flops=1 << 31,
        moved=1 << 23,
    )
    mates = [own_msg] + mates
    base, of_head = call(
        intra_kernel,
        (us, vs, x, local),
        (held((PIECES, 2, C, N), F32), held((LANES, C))),
        [VMEM] * 4,
        [VMEM] * 2,
        flops=1 << 33,
        moved=1 << 23,
    )
    row_totals = call(row_kernel, mates + [base], held((ROW - 1, N + 16, SLICE), F32), [VMEM] * 5, VMEM)
    rows = [send(row_totals[d - 1], along_y(d)) for d in range(1, ROW)]
    back = call(enter_kernel, mates + rows, held((ROW, 2 * N + 16, SLICE), F32), [VMEM] * 7, VMEM)
    shares = [back[0]] + [send(back[e], along_x(e)) for e in range(1, ROW)]
    grads, start, behind, total = call(
        projection_kernel,
        [us, vs, base, half, local, after] + shares,
        (held((ROW,) + chip), held(states), held(states), held((PIECES, LANES), F32)),
        [VMEM] * 10,
        [VMEM] * 4,
        [pltpu.VMEM((2,) + band, F32), pltpu.VMEM(band, F32)],
    )
    returned = [grads[0]] + [lax.ppermute(grads[d], "head", along_z(d)) for d in (1, 3, 2)]
    returned = [returned[0], returned[1], returned[3], returned[2]]
    output, grad_signal, diff = call(
        result_kernel,
        (us, vs, start, behind, x, u2, v2),
        (plain(wide), plain(wide), held(wide)),
        [VMEM] * 7,
        [HBM, HBM, VMEM],
        [pltpu.VMEM((4,) + band, BF16)] * 2 + [pltpu.VMEM((2 * HEADS, LANES), BF16), DMA((4,)), DMA((4,))],
        flops=1 << 34,
        moved=1 << 23,
    )
    decay, totals = call(
        first_decay_kernel,
        (diff, total, of_head),
        (held((HEADS, TOKENS // 2), F32), held((HEADS, PIECES), F32)),
        [VMEM] * 3,
        [VMEM] * 2,
    )
    other = call(swap_kernel, returned + [decay], held((ROW, 2, own, N)), [VMEM] * 5, VMEM)
    other = lax.ppermute(other, "head", OTHER_CORE)
    grad_decay = call(
        decay_kernel, (diff, totals, of_head, decay), plain((HEADS, TOKENS), F32), [VMEM] * 4, VMEM, flops=1 << 31, moved=1 << 22
    )
    narrow = plain(state_in.shape)
    grad_in, grad_out = call(
        join_kernel, returned + [other, far(grad_decay)], (narrow, narrow), [VMEM] * 5 + [HBM], [HBM] * 2, [marks]
    )
    return output, grad_signal, grad_in, grad_out, grad_decay


def solution(mesh):
    in_specs = (
        P("ctx", "head"),
        P("head", "ctx"),
        P(("ctx", "head"), None),
        P(("ctx", "head"), None),
        P("ctx", "head"),
    )
    out_specs = (
        P("ctx", "head"),
        P("ctx", "head"),
        P(("ctx", "head"), None),
        P(("ctx", "head"), None),
        P("head", "ctx"),
    )
    return jax.shard_map(body, mesh=mesh, in_specs=in_specs, out_specs=out_specs, check_vma=False)
```
